128 devices in a mesh: band: 16 (over y, z), tp: 8 (over x, core).
Axes of the slice: x: 4, y: 4, z: 4, core: 2. Of those that a mesh axis runs over, the one named last changes fastest.
Arguments:
- image_in: bfloat16 [8, 1024, 1024], P(None, 'band'), may hold values from -6 to 6
- text_in: bfloat16 [8, 128, 1024], replicated, may hold values from -6 to 6
- text_len: int32 [8], replicated, may hold values from 8 to 128, as said below
- cotangent: bfloat16 [8, 1024, 1024], P(None, 'band'), may hold values from -6 to 6
- gain_one: float32 [1024], replicated, may hold values from 0.1 to 1.9
- w_query: bfloat16 [1024, 1024], P(None, 'tp'), may hold values from -0.1875 to 0.1875
- w_key: bfloat16 [1024, 1024], P(None, 'tp'), may hold values from -0.1875 to 0.1875
- w_value: bfloat16 [1024, 1024], P(None, 'tp'), may hold values from -0.1875 to 0.1875
- w_attn_out: bfloat16 [1024, 1024], P('tp'), may hold values from -0.75 to 0.75
- gain_two: float32 [1024], replicated, may hold values from 0.1 to 1.9
- w_cross_q: bfloat16 [1024, 1024], P(None, 'tp'), may hold values from -0.1875 to 0.1875
- w_cross_k: bfloat16 [1024, 1024], P(None, 'tp'), may hold values from -0.1875 to 0.1875
- w_cross_v: bfloat16 [1024, 1024], P(None, 'tp'), may hold values from -0.1875 to 0.1875
- w_cross_out: bfloat16 [1024, 1024], P('tp'), may hold values from -0.75 to 0.75
- gain_three: float32 [1024], replicated, may hold values from 0.1 to 1.9
- w_hidden: bfloat16 [1024, 4096], P(None, 'tp'), may hold values from -0.1875 to 0.1875
- w_back: bfloat16 [4096, 1024], P('tp'), may hold values from -0.09375 to 0.09375
Outputs:
- layer_out: bfloat16 [8, 1024, 1024], P(None, 'band')
- grad_image: float32 [8, 1024, 1024], P(None, 'band')
- grad_text: float32 [8, 128, 1024], replicated
- grad_gain_one: float32 [1024], replicated
- grad_w_query: float32 [1024, 1024], P(None, 'tp')
- grad_w_key: float32 [1024, 1024], P(None, 'tp')
- grad_w_value: float32 [1024, 1024], P(None, 'tp')
- grad_w_attn_out: float32 [1024, 1024], P('tp')
- grad_gain_two: float32 [1024], replicated
- grad_w_cross_q: float32 [1024, 1024], P(None, 'tp')
- grad_w_cross_k: float32 [1024, 1024], P(None, 'tp')
- grad_w_cross_v: float32 [1024, 1024], P(None, 'tp')
- grad_w_cross_out: float32 [1024, 1024], P('tp')
- grad_gain_three: float32 [1024], replicated
- grad_w_hidden: float32 [1024, 4096], P(None, 'tp')
- grad_w_back: float32 [4096, 1024], P('tp')
The draws below stay inside these ranges and needn't reach their ends.
Inputs may be any that keep to these rules, and one draw needn't show every extreme that they name: Each item's real text tokens are its first text_len positions; in every draw some item has all 128.
All inputs are finite; a program needn't handle non-finite values.
Results may differ from the reference program's by a relative error of at most 0.024.
Values may be sent and summed in bfloat16 or wider, within the bound.
No kernel may reach another device: no remote copies, remote signals or barrier semaphores. Data moves between devices by JAX's collectives and lax.ppermute only.
A program may use at most 320 MiB of HBM per device.

```python
import jax
import jax.numpy as jnp
from jax import lax

D = 1024
HEADS = 16
HD = 64
FF = 4096
TXT = 128
SEQ = 1024
ITEMS = 8


def draw_text_len(key, part):
    key = jax.random.fold_in(key, 11)
    k_pick, k_long, k_short, k_full = jax.random.split(key, 4)
    long_len = jax.random.randint(k_long, (ITEMS,), TXT // 2 + 1, TXT + 1)
    short_len = jax.random.randint(k_short, (ITEMS,), max(TXT // 16, 1), TXT // 2 + 1)
    choose = jax.random.randint(k_pick, (ITEMS,), 0, 4)
    lengths = jnp.where(choose < 3, long_len, short_len)
    full_at = jax.random.randint(k_full, (), 0, ITEMS)
    lengths = jnp.where(jnp.arange(ITEMS) == full_at, TXT, lengths)
    return lengths.astype(jnp.int32)


def block_scale(stream_key, shape, cuts, low, largest):
    def one(axis_at, parts):
        heights = jax.random.uniform(jax.random.fold_in(jax.random.fold_in(stream_key, 6), axis_at), (parts,), jnp.float32, low / len(cuts), largest / len(cuts))
        return jnp.repeat(jnp.exp(heights), shape[axis_at] // parts).reshape((-1,) + (1,) * (len(shape) - axis_at - 1))

    loudness = one(*cuts[0])
    for cut in cuts[1:]:
        loudness = loudness * one(*cut)
    return loudness


def normal_values(stream_key, dims, deviation, most, cuts=(), held_as=jnp.bfloat16):
    gain = block_scale(stream_key, dims, cuts, -0.22, 0.18) if cuts else 1.0
    drawn = jax.random.normal(stream_key, dims, jnp.float32) * deviation * gain
    return jnp.minimum(jnp.maximum(drawn, -most), most).astype(held_as)


def setup_inputs(seed: int = 0) -> dict:
    key_of = jax.random.split(jax.random.key(seed), 18)
    return {
        "image_in": normal_values(key_of[0], (ITEMS, SEQ, D), 1.0, 6.0, ((1, 16),)),
        "text_in": normal_values(key_of[1], (ITEMS, TXT, D), 1.0, 6.0),
        "text_len": draw_text_len(jax.random.fold_in(key_of[17], 71), 0),
        "cotangent": normal_values(key_of[3], (ITEMS, SEQ, D), 1.0, 6.0, ((1, 16),)),
        "gain_one": jnp.clip(1.0 + 0.18 * jax.random.normal(key_of[4], (D,), jnp.float32), 0.1, 1.9),
        "w_query": normal_values(key_of[5], (D, D), D ** -0.5, 0.1875, ((1, 8),)),
        "w_key": normal_values(key_of[6], (D, D), D ** -0.5, 0.1875, ((1, 8),)),
        "w_value": normal_values(key_of[7], (D, D), D ** -0.5, 0.1875, ((1, 8),)),
        "w_attn_out": normal_values(key_of[8], (D, D), (D // 16) ** -0.5, 0.75, ((0, 8),)),
        "gain_two": jnp.clip(1.0 + 0.18 * jax.random.normal(key_of[9], (D,), jnp.float32), 0.1, 1.9),
        "w_cross_q": normal_values(key_of[10], (D, D), D ** -0.5, 0.1875, ((1, 8),)),
        "w_cross_k": normal_values(key_of[11], (D, D), D ** -0.5, 0.1875, ((1, 8),)),
        "w_cross_v": normal_values(key_of[12], (D, D), D ** -0.5, 0.1875, ((1, 8),)),
        "w_cross_out": normal_values(key_of[13], (D, D), (D // 16) ** -0.5, 0.75, ((0, 8),)),
        "gain_three": jnp.clip(1.0 + 0.18 * jax.random.normal(key_of[14], (D,), jnp.float32), 0.1, 1.9),
        "w_hidden": normal_values(key_of[15], (D, FF), D ** -0.5, 0.1875, ((1, 8),)),
        "w_back": normal_values(key_of[16], (FF, D), FF ** -0.5, 0.09375, ((0, 8),)),
    }


@jax.custom_vjp
def low(v):
    return lax.optimization_barrier(v.astype(jnp.bfloat16)).astype(jnp.float32)

@jax.custom_vjp
def low_back(v):
    return v

def low_keep(v):
    return (low(v), None)

def low_pass(kept, grad):
    return (grad,)

def back_keep(v):
    return (v, None)

def back_low(kept, grad):
    return (low(grad),)
low.defvjp(low_keep, low_pass)
low_back.defvjp(back_keep, back_low)
norm_eps = 1e-05
mask_fill = -1000000000.0
highest = lax.Precision.HIGHEST

def gelu_tanh(values):
    inner_arg = 0.7978845608028654 * (values + 0.044715 * values * values * values)
    return 0.5 * values * (1.0 + jnp.tanh(inner_arg))

def layer_norm(values, norm_gain):
    average = lax.optimization_barrier(jnp.mean(values, axis=-1, keepdims=True))
    centred = values - average
    spread = lax.optimization_barrier(jnp.mean(centred * centred, axis=-1, keepdims=True))
    return centred * lax.rsqrt(spread + norm_eps) * norm_gain

def matmul_high(left, right):
    return jnp.dot(left, right, precision=highest)

def both_ways(values):
    return low(low_back(values))

def softmax_rows(scores):
    row_max = lax.optimization_barrier(jnp.max(scores, axis=-1, keepdims=True))
    shifted = jnp.exp(scores - row_max)
    return shifted / lax.optimization_barrier(jnp.sum(shifted, axis=-1, keepdims=True))

def attend_item(queries, key_rows, value_rows, allowed):
    score_scale = HD ** (-0.5)
    scores = low_back(jnp.einsum('qhe,khe->hqk', queries, key_rows, precision=highest) * score_scale)
    scores = jnp.where(allowed, scores, mask_fill)
    prob_rows = low(softmax_rows(scores))
    return both_ways(jnp.einsum('hqk,khe->qhe', prob_rows, value_rows, precision=highest))

def reference(image_in, text_in, text_len, cotangent, gain_one, w_query, w_key, w_value, w_attn_out, gain_two, w_cross_q, w_cross_k, w_cross_v, w_cross_out, gain_three, w_hidden, w_back):
    causal = jnp.arange(SEQ)[None, :] <= jnp.arange(SEQ)[:, None]
    text_pos = jnp.arange(TXT)
    head_shape = (ITEMS, SEQ, HEADS, HD)
    text_shape = (ITEMS, TXT, HEADS, HD)

    def self_block(pieces):
        return attend_item(pieces[0], pieces[1], pieces[2], causal[None])

    def cross_block(pieces):
        allowed = (text_pos < pieces[3])[None, None, :]
        return attend_item(pieces[0], pieces[1], pieces[2], allowed)

    def forward(image_f, text_f, g_one, wq_f, wk_f, wv_f, wo_f, g_two, wcq_f, wck_f, wcv_f, wco_f, g_three, wh_f, wb_f):
        image_rows = image_f.reshape(ITEMS * SEQ, D)
        normed_one = low(layer_norm(image_rows, g_one))
        queries = both_ways(matmul_high(normed_one, wq_f)).reshape(head_shape)
        key_rows = both_ways(matmul_high(normed_one, wk_f)).reshape(head_shape)
        value_rows = both_ways(matmul_high(normed_one, wv_f)).reshape(head_shape)
        self_out = lax.map(jax.checkpoint(self_block), (queries, key_rows, value_rows)).reshape(ITEMS * SEQ, D)
        after_self = image_rows + low_back(matmul_high(self_out, wo_f))
        normed_two = low(layer_norm(after_self, g_two))
        cross_query = both_ways(matmul_high(normed_two, wcq_f)).reshape(head_shape)
        text_rows = text_f.reshape(ITEMS * TXT, D)
        cross_key = both_ways(matmul_high(text_rows, wck_f)).reshape(text_shape)
        cross_value = both_ways(matmul_high(text_rows, wcv_f)).reshape(text_shape)
        cross_out = lax.map(jax.checkpoint(cross_block), (cross_query, cross_key, cross_value, text_len)).reshape(ITEMS * SEQ, D)
        after_cross = after_self + low_back(matmul_high(cross_out, wco_f))
        normed_three = low(layer_norm(after_cross, g_three))
        hidden_low = low(gelu_tanh(low_back(matmul_high(normed_three, wh_f))))
        layer_rows = after_cross + low_back(matmul_high(hidden_low, wb_f))
        return layer_rows.reshape(ITEMS, SEQ, D)
    f32 = jnp.float32
    layer_out, pullback = jax.vjp(forward, image_in.astype(f32), text_in.astype(f32), gain_one, w_query.astype(f32), w_key.astype(f32), w_value.astype(f32), w_attn_out.astype(f32), gain_two, w_cross_q.astype(f32), w_cross_k.astype(f32), w_cross_v.astype(f32), w_cross_out.astype(f32), gain_three, w_hidden.astype(f32), w_back.astype(f32))
    grads = pullback(cotangent.astype(f32))
    return (layer_out.astype(jnp.bfloat16), grads[0], grads[1], grads[2], grads[3], grads[4], grads[5], grads[6], grads[7], grads[8], grads[9], grads[10], grads[11], grads[12], grads[13], grads[14])
```

```python
import jax
import jax.numpy as jnp
from jax import lax
from jax.experimental import pallas as pl
from jax.experimental.pallas import tpu as pltpu
from jax.sharding import PartitionSpec as P

HD = 64
norm_eps = 1e-05
mask_fill = -1000000000.0
BF = jnp.bfloat16
F32 = jnp.float32


def dot(a, b, ca, cb):
    return lax.dot_general(a, b, (((ca,), (cb,)), ((), ())), preferred_element_type=F32)


def gelu_tanh(values):
    inner_arg = 0.7978845608028654 * (values + 0.044715 * values * values * values)
    return 0.5 * values * (1.0 + jnp.tanh(inner_arg))


def norm_parts(rows):
    centred = rows - jnp.mean(rows, axis=-1, keepdims=True)
    inv = lax.rsqrt(jnp.mean(centred * centred, axis=-1, keepdims=True) + norm_eps)
    return centred * inv, inv


def norm_back(rows, gain, grad):
    xh, inv = norm_parts(rows)
    eg = grad * gain
    back = inv * (
        eg
        - jnp.mean(eg, axis=-1, keepdims=True)
        - xh * jnp.mean(eg * xh, axis=-1, keepdims=True)
    )
    return back, jnp.sum((grad * xh).reshape(-1, rows.shape[-1]), axis=0)


def x_shift(v, k):
    return lax.ppermute(v, "tp", [(t, (t + 2 * k) % 8) for t in range(8)])


def core_swap(v):
    return lax.ppermute(v, "tp", [(t, t ^ 1) for t in range(8)])


def gather_tp(v):
    own = jnp.stack([v] + [x_shift(v, k) for k in (1, 2, 3)])
    return jnp.stack([own, core_swap(own)])


def scatter_tp(slots):
    both = (slots[0].astype(F32) + core_swap(slots[1]).astype(F32)).astype(BF)
    total = both[0].astype(F32)
    for k in (1, 2, 3):
        total = total + x_shift(both[k], -k).astype(F32)
    return total


def slot_tp():
    t = lax.axis_index("tp")
    x, core = t // 2, t % 2
    return jnp.stack([((x - k) % 4) * 2 + (core ^ s) for s in (0, 1) for k in range(4)])


def to_item(v):
    perm = [(c * 8 + i, (2 * i + c % 2) * 8 + c // 2) for c in range(16) for i in range(8)]
    return lax.ppermute(v, ("band", "tp"), perm)


def to_band(v):
    perm = [((2 * i + c % 2) * 8 + c // 2, c * 8 + i) for c in range(16) for i in range(8)]
    return lax.ppermute(v, ("band", "tp"), perm)


def z_shift(v, k):
    return lax.ppermute(v, "band", [(b, b // 4 * 4 + (b + k) % 4) for b in range(16)])


def y_shift(v, k):
    return lax.ppermute(v, "band", [(b, (b + 4 * k) % 16) for b in range(16)])


def roll_in(parts, shift):
    return jnp.roll(parts, shift, axis=0)


def sum_band(v):
    return lax.psum(v, "band")


def kernel_call(body, outs, args, smem=0, scratch=(), flops=0, mib=40):
    return pl.pallas_call(
        body,
        out_shape=[jax.ShapeDtypeStruct(s, d) for s, d in outs],
        in_specs=[pl.BlockSpec(memory_space=pltpu.SMEM)] * smem
        + [pl.BlockSpec(memory_space=pltpu.VMEM)] * (len(args) - smem),
        out_specs=[pl.BlockSpec(memory_space=pltpu.VMEM)] * len(outs),
        scratch_shapes=list(scratch),
        compiler_params=pltpu.CompilerParams(vmem_limit_bytes=mib * 2**20),
        cost_estimate=pl.CostEstimate(
            flops=flops,
            bytes_accessed=sum(a.size * a.dtype.itemsize for a in args),
            transcendentals=0,
        ),
    )(*args)


def head_rows(v):
    first = lax.broadcasted_iota(jnp.int32, v.shape, 1) < 64
    zero = jnp.zeros_like(v)
    return jnp.concatenate([jnp.where(first, v, zero), jnp.where(first, zero, v)], axis=0)


def head_cols(v):
    r = v.shape[0] // 2
    first = lax.broadcasted_iota(jnp.int32, (r, 128), 1) < 64
    return jnp.where(first, v[:r], v[r:])


def soft(s):
    e = jnp.exp(s - jnp.max(s, axis=-1, keepdims=True))
    return (e / jnp.sum(e, axis=-1, keepdims=True)).astype(BF)


def soft_back(p, dp):
    pf = p.astype(F32)
    return (pf * (dp - jnp.sum(dp * pf, axis=-1, keepdims=True))).astype(BF)


def qkv_body(image, gain, wq, wk, wv, a1, send):
    for i in range(8):
        xh, _ = norm_parts(image[i].astype(F32))
        a1[i * 64 : i * 64 + 64] = (xh * gain[...]).astype(BF)
    w = jnp.concatenate([wq[...], wk[...], wv[...]], axis=1)
    qkv = dot(a1[...], w, 1, 0).astype(BF).reshape(8, 64, 384)
    for i in range(8):
        send[2 * i] = qkv[i]
        send[2 * i + 1] = qkv[i]


def attend_body(par_ref, got, cols, probs):
    par = par_ref[0]
    for j in range(8):
        n = 128 * (j + 1)
        q = head_rows(got[2 * j + par, :, 0:128])
        k = got[0 : 2 * j + 2, :, 128:256].reshape(n, 128)
        v = got[0 : 2 * j + 2, :, 256:384].reshape(n, 128)
        s = dot(q, k, 1, 1) * 0.125
        row = lax.broadcasted_iota(jnp.int32, (128, n), 0) % 64 + (128 * j + 64 * par)
        s = jnp.where(lax.broadcasted_iota(jnp.int32, (128, n), 1) <= row, s, mask_fill)
        p = soft(s)
        probs[j, :, 0:n] = p
        cols[j] = head_cols(dot(p, v, 1, 0)).astype(BF)


def attend_back_body(par_ref, got, probs, dheads, send, dk, dv):
    par = par_ref[0]
    dk[...] = jnp.zeros_like(dk)
    dv[...] = jnp.zeros_like(dv)
    for j in range(8):
        n = 128 * (j + 1)
        q = head_rows(got[2 * j + par, :, 0:128])
        k = got[0 : 2 * j + 2, :, 128:256].reshape(n, 128)
        v = got[0 : 2 * j + 2, :, 256:384].reshape(n, 128)
        g = head_rows(dheads[j])
        p = probs[j, :, 0:n]
        ds = soft_back(p, dot(g, v, 1, 1))
        dv[0:n] += dot(p, g, 0, 0)
        dk[0:n] += dot(ds, q, 0, 0)
        send[2 * j + par, :, 0:128] = (head_cols(dot(ds, k, 1, 0)) * 0.125).astype(BF)
        send[2 * j + 1 - par, :, 0:128] = jnp.zeros((64, 128), BF)
    send[:, :, 128:256] = (dk[...] * 0.125).astype(BF).reshape(16, 64, 128)
    send[:, :, 256:384] = dv[...].astype(BF).reshape(16, 64, 128)


def middle_body(slots, tlen, heads, image, gain2, gain3, *refs):
    w, (after_self, a2, cq, probs, cross, cross_abs, after_cross, a3) = refs[:8], refs[8:]
    acc = image[...].astype(F32)
    for s in range(8):
        acc += dot(heads[slots[s]], w[s][:, 0:1024], 1, 0)
    after_self[...] = acc
    xh, _ = norm_parts(acc)
    a2[...] = (xh * gain2[...]).astype(BF)
    live = lax.broadcasted_iota(jnp.int32, (128, 128), 1) < tlen[0]
    for s in range(8):
        cqs = dot(a2[...], w[s][:, 1024:2048], 1, 1).astype(BF)
        cq[s] = cqs
        sc = dot(head_rows(cqs), w[s][:, 3072:3200], 1, 0) * 0.125
        p = soft(jnp.where(live, sc, mask_fill))
        probs[s] = p
        cs = head_cols(dot(p, w[s][:, 3200:3328], 1, 1)).astype(BF)
        cross[s] = cs
        cross_abs[slots[s]] = cs
    acc = after_self[...]
    for s in range(8):
        acc += dot(cross[s], w[s][:, 2048:3072], 1, 0)
    after_cross[...] = acc
    xh, _ = norm_parts(acc)
    a3[...] = (xh * gain3[...]).astype(BF)


def middle_back_body(slots, e0, e1, e2, e3, cot, after_cross, after_self, cq, probs, gain2, gain3, *refs):
    w, (g2l, g1l, dcq, dckv, dself, dgain, g2) = refs[:8], refs[8:]
    e = (e0[...].astype(F32) + e2[...].astype(F32)) + (e1[...].astype(F32) + e3[...].astype(F32))
    back, dg3 = norm_back(after_cross[...], gain3[...], e)
    g2[...] = cot[...].astype(F32) + back
    g2l[...] = g2[...].astype(BF)
    da2 = jnp.zeros((64, 1024), F32)
    for s in range(8):
        dc = head_rows(dot(g2l[...], w[s][:, 2048:3072], 1, 1).astype(BF))
        p = probs[s]
        ds = soft_back(p, dot(dc, w[s][:, 3200:3328], 1, 0))
        dq = (head_cols(dot(ds, w[s][:, 3072:3200], 1, 1)) * 0.125).astype(BF)
        dcq[slots[s]] = dq
        dk = dot(head_rows(cq[s]), ds, 0, 0) * 0.125
        dv = dot(dc, p, 0, 0)
        dckv[slots[s]] = jnp.concatenate([dk, dv], axis=1).astype(BF)
        da2 += dot(dq, w[s][:, 1024:2048], 1, 0)
    back, dg2 = norm_back(after_self[...], gain2[...], da2)
    g1l[...] = (g2[...] + back).astype(BF)
    dgain[0:1] = dg2.reshape(1, 1024)
    dgain[1:2] = dg3.reshape(1, 1024)
    for s in range(8):
        dself[slots[s]] = dot(g1l[...], w[s][:, 0:1024], 1, 1).astype(BF)


def hidden_body(a0, a1, a2, a3, other, dact, wh, hid, dpre, da_own, da_other, a3_all):
    for k, a in enumerate((a0, a1, a2, a3)):
        a3_all[64 * k : 64 * k + 64] = a[...]
        a3_all[256 + 64 * k : 320 + 64 * k] = other[k]
    for r in range(4):
        rows = slice(128 * r, 128 * r + 128)
        u = dot(a3_all[rows], wh[...], 1, 0)
        th = jnp.tanh(0.7978845608028654 * (u + 0.044715 * u * u * u))
        hid[rows] = (0.5 * u * (1.0 + th)).astype(BF)
        slope = 0.5 * (1.0 + th) + 0.5 * u * (1.0 - th * th) * (
            0.7978845608028654 * (1.0 + 0.134145 * u * u)
        )
        dpre[rows] = (dact[rows] * slope).astype(BF)
        part = dot(dpre[rows], wh[...], 1, 1).astype(BF).reshape(2, 64, 1024)
        ref = da_own if r < 2 else da_other
        ref[2 * (r % 2) : 2 * (r % 2) + 2] = part


def first_body(slots, got, wq, wk, wv, dqkv, own, other, ordered):
    for i in range(8):
        both = got[2 * i].astype(F32) + got[2 * i + 1].astype(F32)
        dqkv[64 * i : 64 * i + 64] = both.astype(BF)
    for s in range(8):
        start = pl.multiple_of(slots[s] * 64, 64)
        ordered[64 * s : 64 * s + 64] = dqkv[pl.ds(start, 64)]
    w = jnp.concatenate([wq[...], wk[...], wv[...]], axis=1)
    own[...] = dot(ordered[0:256], w, 1, 1).astype(BF).reshape(4, 64, 1024)
    other[...] = dot(ordered[256:512], w, 1, 1).astype(BF).reshape(4, 64, 1024)


def image_body(e0, e1, e2, e3, image, gain, g1, gimg):
    e = (e0[...].astype(F32) + e2[...].astype(F32)) + (e1[...].astype(F32) + e3[...].astype(F32))
    xh, inv = norm_parts(image[...].astype(F32))
    eg = e * gain[...]
    back = inv * (
        eg
        - jnp.mean(eg, axis=-1, keepdims=True)
        - xh * jnp.mean(eg * xh, axis=-1, keepdims=True)
    )
    gimg[...] = (g1[...].astype(F32) + back).astype(BF)


def place_body(slots, a0, a1, a2, a3, other, out):
    for k, a in enumerate((a0, a1, a2, a3)):
        out[slots[k]] = a[...].astype(out.dtype)
        out[slots[4 + k]] = other[k].astype(out.dtype)


def shifts(v):
    return [v] + [x_shift(v, k) for k in (1, 2, 3)]


def gather_parts(v):
    own = shifts(v)
    return own, core_swap(jnp.stack(own))


def scatter_parts(own, other):
    got = core_swap(other)
    both = [(own[k].astype(F32) + got[k].astype(F32)).astype(BF) for k in range(4)]
    return [both[0]] + [x_shift(both[k], -k) for k in (1, 2, 3)]


def sum_all(v):
    for move in (z_shift, y_shift, x_shift):
        v = (v + move(v, 2)) + (move(v, 1) + move(v, 3))
    return v + core_swap(v)


def gather_band(v):
    rows = [v] + [z_shift(v, k) for k in (1, 2, 3)]
    rows = jnp.stack(rows)
    return jnp.stack([rows] + [y_shift(rows, k) for k in (1, 2, 3)])


def slot_band():
    b = lax.axis_index("band")
    y, z = b // 4, b % 4
    return jnp.stack([((y - j) % 4) * 4 + (z - k) % 4 for j in range(4) for k in range(4)])


def reduce_band(v):
    got = lax.all_to_all(v, "band", 0, 0).astype(F32)
    return gather_band(jnp.sum(got, axis=0).astype(BF))


def place_three_body(slots, parts, o0, o1, o2):
    for s in range(16):
        start = pl.multiple_of(slots[s] * 64, 64)
        block = parts[s // 4, s % 4]
        for c, o in enumerate((o0, o1, o2)):
            o[pl.ds(start, 64)] = block[:, 128 * c : 128 * c + 128].astype(F32)


def place_five_body(slots, parts, o0, o1, o2, o3, o4):
    for s in range(16):
        start = pl.multiple_of(slots[s] * 64, 64)
        block = parts[s // 4, s % 4].astype(F32)
        for c, o in enumerate((o0, o1, o2)):
            o[pl.ds(start, 64)] = block[:, 128 * c : 128 * c + 128]
        start = pl.multiple_of(slots[s] * 8, 8)
        for c, o in enumerate((o3, o4)):
            cols = block[:, 384 + 128 * c : 512 + 128 * c]
            for m in range(8):
                o[pl.ds(start, 8), 128 * m : 128 * m + 128] = cols[8 * m : 8 * m + 8]


def local(
    image_in,
    text_in,
    text_len,
    cotangent,
    gain_one,
    w_query,
    w_key,
    w_value,
    w_attn_out,
    gain_two,
    w_cross_q,
    w_cross_k,
    w_cross_v,
    w_cross_out,
    gain_three,
    w_hidden,
    w_back,
):
    band, tp = lax.axis_index("band"), lax.axis_index("tp")
    item, par = band // 2, (band % 2).reshape(1)
    slots, bslots = slot_tp(), slot_band()
    pick = lambda a, i: lax.dynamic_index_in_dim(a, i, 0, False)
    row = lambda g: g.reshape(1, 1024)
    chunk = ((64, 1024), BF)

    text = pick(text_in, item)
    ckT = dot(w_cross_k, text, 0, 1).astype(BF)
    cvT = dot(w_cross_v, text, 0, 1).astype(BF)
    wbuf = jnp.concatenate([w_attn_out, w_cross_q.T, w_cross_out, ckT, cvT], axis=1)
    w_own = shifts(wbuf)
    w_all = w_own + [core_swap(v) for v in w_own]
    image_own = pick(image_in, tp)
    moved = to_item(jnp.stack([image_own, pick(cotangent, tp)]))
    image_c, cot_c = moved[0], moved[1]
    cot_own, cot_other = gather_parts(cot_c)
    cot_all = jnp.concatenate([jnp.stack(cot_own), cot_other]).reshape(512, 1024)
    dact = dot(cot_all, w_back, 1, 1)

    a1, send = kernel_call(
        qkv_body,
        [((512, 1024), BF), ((16, 64, 384), BF)],
        [image_in, row(gain_one), w_query, w_key, w_value],
        flops=402653184,
    )
    got = lax.all_to_all(send, "band", 0, 0)
    self_cols, probs = kernel_call(
        attend_body,
        [((8, 64, 128), BF), ((8, 128, 1024), BF)],
        [par, got],
        smem=1,
        flops=300000000,
    )
    heads = lax.all_to_all(self_cols, "tp", 0, 0)

    after_self, a2, cq, cprobs, cross, cross_abs, after_cross, a3 = kernel_call(
        middle_body,
        [
            ((64, 1024), F32),
            chunk,
            ((8, 64, 128), BF),
            ((8, 128, 128), BF),
            ((8, 64, 128), BF),
            ((8, 64, 128), BF),
            ((64, 1024), F32),
            chunk,
        ],
        [slots, text_len[item].reshape(1), heads, image_c, row(gain_two), row(gain_three), *w_all],
        smem=2,
        flops=500000000,
    )

    a3_own, a3_other = gather_parts(a3)
    hid, dpre, da_own, da_other, a3_all = kernel_call(
        hidden_body,
        [
            ((512, 512), BF),
            ((512, 512), BF),
            ((4, 64, 1024), BF),
            ((4, 64, 1024), BF),
            ((512, 1024), BF),
        ],
        [*a3_own, a3_other, dact, w_hidden],
        flops=1073741824,
    )
    da3 = scatter_parts(da_own, da_other)
    out_part = dot(hid, w_back, 1, 0).astype(BF).reshape(2, 4, 64, 1024)
    dw_back = dot(hid, cot_all, 0, 0)
    dw_hidden = dot(a3_all, dpre, 0, 0)

    g2_low, g1_low, dcq, dckv, dself, dgain23 = kernel_call(
        middle_back_body,
        [
            chunk,
            chunk,
            ((8, 64, 128), BF),
            ((8, 128, 256), BF),
            ((8, 64, 128), BF),
            ((2, 1024), F32),
        ],
        [slots, *da3, cot_c, after_cross, after_self, cq, cprobs, row(gain_two), row(gain_three)]
        + w_all,
        smem=1,
        scratch=[pltpu.VMEM((64, 1024), F32)],
        flops=700000000,
    )

    out_parts = scatter_parts(out_part[0], out_part[1])
    layer_c = (after_cross + sum(v.astype(F32) for v in out_parts)).astype(BF)

    dheads = lax.all_to_all(dself, "tp", 0, 0)
    (send,) = kernel_call(
        attend_back_body,
        [((16, 64, 384), BF)],
        [par, got, probs, dheads],
        smem=1,
        scratch=[pltpu.VMEM((1024, 128), F32)] * 2,
        flops=700000000,
    )
    got = lax.all_to_all(send, "band", 0, 0)
    dqkv, e_own, e_other = kernel_call(
        first_body,
        [((512, 384), BF), ((4, 64, 1024), BF), ((4, 64, 1024), BF)],
        [slots, got, w_query, w_key, w_value],
        smem=1,
        scratch=[pltpu.VMEM((512, 384), BF)],
        flops=402653184,
    )
    e1 = scatter_parts(e_own, e_other)
    dw_qkv = dot(a1, dqkv, 0, 0)
    w_qkv = jnp.concatenate([w_query, w_key, w_value], axis=1)
    dgain1 = jnp.sum(dw_qkv * w_qkv.astype(F32), axis=1) / gain_one
    moved = to_band(jnp.stack([g1_low, layer_c]))
    (gimg,) = kernel_call(
        image_body, [chunk], [*e1, image_own, row(gain_one), moved[0]], flops=1000000
    )
    place = lambda own, other, kind: kernel_call(
        place_body, [((8, 64, 1024), kind)], [slots, *own, other], smem=1, flops=1000000
    )[0]
    gimg = place(*gather_parts(gimg), F32)
    layer_out = place(*gather_parts(moved[1]), BF)

    wg_own, wg_other = gather_parts(jnp.concatenate([a2, g2_low, g1_low], axis=1))
    wg = jnp.concatenate([jnp.stack(wg_own), wg_other]).reshape(512, 3072)
    cols = lax.all_to_all(jnp.concatenate([cross_abs, dcq], axis=2), "tp", 0, 0)
    cols = jnp.take(jnp.concatenate([cols, self_cols], axis=2), slots, axis=0).reshape(512, 384)
    dw_cross_out = dot(cols[:, :128], wg[:, 1024:2048], 0, 0)
    dw_cross_q = dot(wg[:, :1024], cols[:, 128:256], 0, 0)
    dw_attn_out = dot(cols[:, 256:], wg[:, 2048:], 0, 0)

    dckv = jnp.sum(lax.all_to_all(dckv, "tp", 0, 0).astype(F32), axis=0)
    pair = [(b, b ^ 1) for b in range(16)]
    dckv = dckv.astype(BF)
    dckv = (dckv.astype(F32) + lax.ppermute(dckv, "band", pair).astype(F32)).astype(BF)
    dw_cross_k = dot(text, dckv[:, :128], 0, 1) * 0.5
    dw_cross_v = dot(text, dckv[:, 128:], 0, 1) * 0.5
    half = lax.dynamic_index_in_dim(dckv.reshape(128, 2, 2, 64), par[0], 2, False)
    tpart = dot(half[:, 0], w_cross_k, 0, 1) + dot(half[:, 1], w_cross_v, 0, 1)
    tsum = jnp.sum(
        lax.all_to_all(tpart.astype(BF).reshape(8, 8, 1024), "tp", 0, 0).astype(F32), axis=0
    )
    grad_text = lax.all_gather(tsum.astype(BF), ("band", "tp"), axis=0, tiled=True)
    grad_text = grad_text.astype(F32).reshape(8, 128, 1024)

    dgains = sum_all(jnp.concatenate([dgain1.reshape(1, 1024), dgain23]))
    dw_back, dw_hidden = (
        v.astype(F32) for v in lax.psum((dw_back.astype(BF), dw_hidden.astype(BF)), "band")
    )
    fold = lambda v: v.reshape(16, 8, 8, 128).transpose(0, 2, 1, 3).reshape(16, 64, 128)
    fold_rows = lambda v: v.reshape(16, 64, 128)
    mid = jnp.concatenate(
        [
            fold_rows(dw_cross_q),
            fold_rows(dw_cross_k),
            fold_rows(dw_cross_v),
            fold(dw_attn_out),
            fold(dw_cross_out),
        ],
        axis=2,
    ).astype(BF)
    tall, wide = ((1024, 128), F32), ((128, 1024), F32)
    dw_cross_q, dw_cross_k, dw_cross_v, dw_attn_out, dw_cross_out = kernel_call(
        place_five_body, [tall, tall, tall, wide, wide], [bslots, reduce_band(mid)], smem=1, flops=1
    )
    dw_query, dw_key, dw_value = kernel_call(
        place_three_body,
        [tall, tall, tall],
        [bslots, reduce_band(dw_qkv.astype(BF).reshape(16, 64, 384))],
        smem=1,
        flops=1,
    )
    return (
        layer_out,
        gimg,
        grad_text,
        dgains[0],
        dw_query,
        dw_key,
        dw_value,
        dw_attn_out,
        dgains[1],
        dw_cross_q,
        dw_cross_k,
        dw_cross_v,
        dw_cross_out,
        dgains[2],
        dw_hidden,
        dw_back,
    )


def solution(mesh):
    rows, cols, heads = P(None, "band", None), P(None, "tp"), P("tp", None)
    in_specs = (
        rows, P(), P(), rows, P(), cols, cols, cols, heads, P(), cols, cols, cols, heads, P(), cols, heads,
    )
    out_specs = (
        rows, rows, P(), P(), cols, cols, cols, heads, P(), cols, cols, cols, heads, P(), cols, heads,
    )
    return jax.shard_map(local, mesh=mesh, in_specs=in_specs, out_specs=out_specs, check_vma=False)
```

```python
import jax
import jax.numpy as jnp
from jax import lax
from jax.experimental import pallas as pl
from jax.experimental.pallas import tpu as pltpu
from jax.sharding import PartitionSpec as P

HD = 64
norm_eps = 1e-05
mask_fill = -1000000000.0
BF = jnp.bfloat16
F32 = jnp.float32


def dot(a, b, ca, cb):
    return lax.dot_general(a, b, (((ca,), (cb,)), ((), ())), preferred_element_type=F32)


def norm_parts(rows):
    centred = rows - jnp.mean(rows, axis=-1, keepdims=True)
    inv = lax.rsqrt(jnp.mean(centred * centred, axis=-1, keepdims=True) + norm_eps)
    return centred * inv, inv


def norm_back(rows, gain, grad):
    xh, inv = norm_parts(rows)
    eg = grad * gain
    back = inv * (
        eg
        - jnp.mean(eg, axis=-1, keepdims=True)
        - xh * jnp.mean(eg * xh, axis=-1, keepdims=True)
    )
    return back, jnp.sum((grad * xh).reshape(-1, rows.shape[-1]), axis=0)


def x_shift(v, k):
    return lax.ppermute(v, "tp", [(t, (t + 2 * k) % 8) for t in range(8)])


def core_swap(v):
    return lax.ppermute(v, "tp", [(t, t ^ 1) for t in range(8)])


def z_shift(v, k):
    return lax.ppermute(v, "band", [(b, b // 4 * 4 + (b + k) % 4) for b in range(16)])


def y_shift(v, k):
    return lax.ppermute(v, "band", [(b, (b + 4 * k) % 16) for b in range(16)])


def gather_band(v):
    rows = jnp.stack([v] + [z_shift(v, k) for k in (1, 2, 3)])
    return jnp.stack([rows] + [y_shift(rows, k) for k in (1, 2, 3)])


def to_item(v):
    perm = [(c * 8 + i, (2 * i + c % 2) * 8 + c // 2) for c in range(16) for i in range(8)]
    return lax.ppermute(v, ("band", "tp"), perm)


def to_band(v):
    perm = [((2 * i + c % 2) * 8 + c // 2, c * 8 + i) for c in range(16) for i in range(8)]
    return lax.ppermute(v, ("band", "tp"), perm)


def kernel_call(body, outs, args, smem=1, scratch=(), mib=40, us=0):
    def whole(shape):
        return pl.BlockSpec(
            shape, lambda *_: (0,) * len(shape), pipeline_mode=pl.Buffered(buffer_count=1)
        )

    def block(arg):
        if not isinstance(arg, tuple):
            return whole(arg.shape)
        array, first, place = arg
        rest = array.shape[1:]
        return pl.BlockSpec(
            (first, *rest),
            lambda _, *scalars: (place(*scalars), *(0 for _ in rest)),
            pipeline_mode=pl.Buffered(buffer_count=1),
        )

    arrays = [a[0] if isinstance(a, tuple) else a for a in args]
    return pl.pallas_call(
        body,
        out_shape=[jax.ShapeDtypeStruct(s, d) for s, d in outs],
        grid_spec=pltpu.PrefetchScalarGridSpec(
            num_scalar_prefetch=smem,
            grid=(1,),
            in_specs=[block(a) for a in args[smem:]],
            out_specs=[whole(s) for s, _ in outs],
            scratch_shapes=list(scratch),
        ),
        compiler_params=pltpu.CompilerParams(vmem_limit_bytes=mib * 2**20),
        cost_estimate=pl.CostEstimate(
            flops=1, bytes_accessed=1 + us * 3700000, transcendentals=0
        ),
    )(*arrays)


def of_item(v):
    return (v, 1, lambda ids, *_: lax.div(ids[0], 2))


def of_tp(v):
    return (v, 1, lambda ids, *_: ids[1])


def slot(ids, s):
    t = ids[1]
    x = lax.rem(lax.div(t, 2) + 4 - s % 4, 4)
    core = lax.rem(t + s // 4, 2)
    return 2 * x + core


def side(ids, s, x):
    return 2 * x + lax.rem(ids[1] + s, 2)


def band_slot(ids, n):
    y, z = lax.div(ids[0], 4), lax.rem(ids[0], 4)
    return 4 * lax.rem(y + 4 - n // 4, 4) + lax.rem(z + 4 - n % 4, 4)


def head_rows(v):
    first = lax.broadcasted_iota(jnp.int32, v.shape, 1) < 64
    zero = jnp.zeros_like(v)
    return jnp.concatenate([jnp.where(first, v, zero), jnp.where(first, zero, v)], axis=0)


def head_cols(v):
    r = v.shape[0] // 2
    first = lax.broadcasted_iota(jnp.int32, (r, 128), 1) < 64
    return jnp.where(first, v[:r], v[r:])


def soft(s):
    e = jnp.exp(s - jnp.max(s, axis=-1, keepdims=True))
    return (e / jnp.sum(e, axis=-1, keepdims=True)).astype(BF)


def soft_back(p, dp):
    pf = p.astype(F32)
    return (pf * (dp - jnp.sum(dp * pf, axis=-1, keepdims=True))).astype(BF)


def sum_four(e0, e1, e2, e3):
    return (e0[...].astype(F32) + e2[...].astype(F32)) + (
        e1[...].astype(F32) + e3[...].astype(F32)
    )


def fold(v):
    return jnp.concatenate([v[:, 128 * m : 128 * m + 128] for m in range(8)], axis=0)


def qkv_body(ids, image, gain, wq, wk, wv, send, own, a1):
    own[...] = image[ids[1]]
    for i in range(8):
        xh, _ = norm_parts(image[i].astype(F32))
        a1[i * 64 : i * 64 + 64] = (xh * gain[...]).astype(BF)
    w = jnp.concatenate([wq[...], wk[...], wv[...]], axis=1)
    qkv = dot(a1[...], w, 1, 0).astype(BF).reshape(8, 64, 384)
    cols = pl.ds(pl.multiple_of(ids[1] * 128, 128), 128)
    for i in range(8):
        part = image[i, :, cols]
        for p in (0, 1):
            send[2 * i + p, :, 0:384] = qkv[i]
            send[2 * i + p, :, 384:512] = part


def prep_body(ids, text, wcq, wck, wcv, wco, buf):
    mine = text[0]
    buf[:, 0:1024] = jnp.transpose(wcq[...].astype(F32)).astype(BF)
    buf[:, 1024:2048] = wco[...]
    buf[:, 2048:2176] = dot(wck[...], mine, 0, 1).astype(BF)
    buf[:, 2176:2304] = dot(wcv[...], mine, 0, 1).astype(BF)


def attend_body(ids, got, wo, cols, probs, own, other):
    par = lax.rem(ids[0], 2)
    for j in range(8):
        n = 128 * (j + 1)
        q = head_rows(got[2 * j + par, :, 0:128])
        k = got[0 : 2 * j + 2, :, 128:256].reshape(n, 128)
        v = got[0 : 2 * j + 2, :, 256:384].reshape(n, 128)
        s = dot(q, k, 1, 1) * 0.125
        row = lax.broadcasted_iota(jnp.int32, (128, n), 0) % 64 + (128 * j + 64 * par)
        s = jnp.where(lax.broadcasted_iota(jnp.int32, (128, n), 1) <= row, s, mask_fill)
        p = soft(s)
        probs[j, :, 0:n] = p
        cols[j] = head_cols(dot(p, v, 1, 0)).astype(BF)
    mine = pl.ds(pl.multiple_of(ids[1] * 128, 128), 128)
    for ref, first in ((other, 4), (own, 0)):
        c = jnp.concatenate([cols[slot(ids, first + k)] for k in range(4)], axis=0)
        ref[...] = dot(c, wo[...], 1, 0).astype(BF).reshape(4, 64, 1024)
        part = dot(c, wo[:, mine], 1, 0)
        for k in range(4):
            res = got[2 * slot(ids, first + k) + par, :, 384:512].astype(F32)
            ref[k, :, mine] = (part[64 * k : 64 * k + 64] + res).astype(BF)


def attend_back_body(
    ids, got, probs, wo, a0, a1, a2, a3, others, dq, kv_own, kv_other, g1, dk, dv, dheads
):
    par = lax.rem(ids[0], 2)
    for k, a in enumerate((a0, a1, a2, a3)):
        g1[slot(ids, k)] = a[...]
        g1[slot(ids, 4 + k)] = others[k]
    dheads[...] = dot(g1[...].reshape(512, 1024), wo[...], 1, 1).astype(BF).reshape(8, 64, 128)
    dk[...] = jnp.zeros_like(dk)
    dv[...] = jnp.zeros_like(dv)
    for j in range(8):
        n = 128 * (j + 1)
        q = head_rows(got[2 * j + par, :, 0:128])
        k = got[0 : 2 * j + 2, :, 128:256].reshape(n, 128)
        v = got[0 : 2 * j + 2, :, 256:384].reshape(n, 128)
        g = head_rows(dheads[j])
        p = probs[j, :, 0:n]
        ds = soft_back(p, dot(g, v, 1, 1))
        dv[0:n] += dot(p, g, 0, 0)
        dk[0:n] += dot(ds, q, 0, 0)
        dq[j] = (head_cols(dot(ds, k, 1, 0)) * 0.125).astype(BF)
    for j in range(8):
        own = pl.ds(pl.multiple_of(128 * j + 64 * par, 64), 64)
        other = pl.ds(pl.multiple_of(128 * j + 64 - 64 * par, 64), 64)
        kv_own[j, :, 0:128] = dk[own] * 0.125
        kv_own[j, :, 128:256] = dv[own]
        kv_other[j, :, 0:128] = (dk[other] * 0.125).astype(BF)
        kv_other[j, :, 128:256] = dv[other].astype(BF)


def split_weights(refs):
    halves = []
    for first in (0, 5):
        a, b, q, o, c = refs[first : first + 5]
        cut = [(r.at[:, 0:1024], r.at[:, 1024:2304]) for r in (a, b, c)]
        halves += [cut[0], cut[1], (q, o), cut[2]]
    return [h[0] for h in halves], [h[1] for h in halves]


def middle_body(ids, tlen, e0, e1, e2, e3, gain2, gain3, *refs):
    (wq, wo), outs = split_weights(refs[:10]), refs[10:]
    after_self, a2, cq, probs, cross, after_cross, a3 = outs
    acc = sum_four(e0, e1, e2, e3)
    after_self[...] = acc
    xh, _ = norm_parts(acc)
    a2[...] = (xh * gain2[...]).astype(BF)
    live = lax.broadcasted_iota(jnp.int32, (128, 128), 1) < tlen[lax.div(ids[0], 2)]
    for s in range(8):
        cqs = dot(a2[...], wq[s][...], 1, 1).astype(BF)
        cq[s] = cqs
        sc = dot(head_rows(cqs), wo[s][:, 1024:1152], 1, 0) * 0.125
        p = soft(jnp.where(live, sc, mask_fill))
        probs[s] = p
        cross[s] = head_cols(dot(p, wo[s][:, 1152:1280], 1, 1)).astype(BF)
    acc = after_self[...]
    for s in range(8):
        acc += dot(cross[s], wo[s][:, 0:1024], 1, 0)
    after_cross[...] = acc
    xh, _ = norm_parts(acc)
    a3[...] = (xh * gain3[...]).astype(BF)


def middle_back_body(ids, parts, cot, after_cross, after_self, cq, probs, cross, image, gain1, gain2, gain3, *refs):
    (wq, wo), (both, g1_low, g1, cols, dgain, g2) = split_weights(refs[:10]), refs[10:]
    e = sum_four(*(parts.at[x] for x in range(4)))
    back, dg3 = norm_back(after_cross[...], gain3[...], e)
    g2[...] = cot[0].astype(F32) + back
    g2l = g2[...].astype(BF)
    both[:, 1024:2048] = g2l
    xh, _ = norm_parts(image[...].astype(F32))
    both[:, 2048:3072] = (xh * gain1[...]).astype(BF)
    da2 = jnp.zeros((64, 1024), F32)
    for s in range(8):
        dc = head_rows(dot(g2l, wo[s][:, 0:1024], 1, 1).astype(BF))
        p = probs[s]
        ds = soft_back(p, dot(dc, wo[s][:, 1152:1280], 1, 0))
        dq = (head_cols(dot(ds, wo[s][:, 1024:1152], 1, 1)) * 0.125).astype(BF)
        dk = dot(head_rows(cq[s]), ds, 0, 0) * 0.125
        dv = dot(dc, p, 0, 0)
        to = slot(ids, s)
        cols[to, 0:64, 0:128] = cross[s]
        cols[to, 0:64, 128:256] = dq
        cols[to, 64:192, 0:128] = dk.astype(BF)
        cols[to, 64:192, 128:256] = dv.astype(BF)
        da2 += dot(dq, wq[s][...], 1, 0)
    v = after_self[...]
    xh, _ = norm_parts(v)
    both[:, 0:1024] = (xh * gain2[...]).astype(BF)
    back, dg2 = norm_back(v, gain2[...], da2)
    g1[...] = g2[...] + back
    g1l = g1[...].astype(BF)
    g1_low[...] = g1l
    dgain[0:8] = jnp.concatenate([dg2[128 * m : 128 * m + 128].reshape(1, 128) for m in range(8)])
    dgain[8:16] = jnp.concatenate([dg3[128 * m : 128 * m + 128].reshape(1, 128) for m in range(8)])


def hidden_body(ids, a0, a1, a2, a3, others, dact, wh, hid, dpre, da_own, da_other, a3_all):
    for k, a in enumerate((a0, a1, a2, a3)):
        a3_all[slot(ids, k)] = a[...]
        a3_all[slot(ids, 4 + k)] = others[k]
    for r in range(4):
        rows = slice(128 * r, 128 * r + 128)
        u = dot(a3_all[2 * r : 2 * r + 2].reshape(128, 1024), wh[...], 1, 0)
        th = jnp.tanh(0.7978845608028654 * (u + 0.044715 * u * u * u))
        hid[rows] = (0.5 * u * (1.0 + th)).astype(BF)
        slope = 0.5 * (1.0 + th) + 0.5 * u * (1.0 - th * th) * (
            0.7978845608028654 * (1.0 + 0.134145 * u * u)
        )
        dpre[2 * r : 2 * r + 2] = (dact[rows] * slope).astype(BF).reshape(2, 64, 512)
    for ref, s in ((da_other, 1), (da_own, 0)):
        d = jnp.concatenate([dpre[side(ids, s, x)] for x in range(4)], axis=0)
        ref[...] = dot(d, wh[...], 1, 1).astype(BF).reshape(4, 64, 1024)


def hidden_grad_body(ids, hid, dpre, a3_all, cot, wb, own, other, dwb, dwh, part):
    h = hid[...]
    part[...] = dot(h, wb[...], 1, 0).astype(BF).reshape(8, 64, 1024)
    for k in range(4):
        own[k] = part[slot(ids, k)]
        other[k] = part[slot(ids, 4 + k)]
    dwb[...] = dot(h, cot[...].reshape(512, 1024), 0, 0)
    dwh[...] = dot(a3_all[...].reshape(512, 1024), dpre[...].reshape(512, 512), 0, 0)


def first_body(ids, dq, kv_own, kv_got, wq, wk, wv, dqkv, own, other):
    for j in range(8):
        dqkv[j, :, 0:128] = dq[j]
        dqkv[j, :, 128:384] = (kv_own[j] + kv_got[j].astype(F32)).astype(BF)
    w = jnp.concatenate([wq[...], wk[...], wv[...]], axis=1)
    for ref, first in ((other, 4), (own, 0)):
        d = jnp.concatenate([dqkv[slot(ids, first + k)] for k in range(4)], axis=0)
        ref[...] = dot(d, w, 1, 1).astype(BF).reshape(4, 64, 1024)


def copy_body(ids, dwb, dwh, out_b, out_h):
    out_b[...] = dwb[...]
    out_h[...] = dwh[...]


def layer_body(ids, p0, p1, p2, p3, after_cross, out):
    out[...] = (after_cross[...] + sum_four(p0, p1, p2, p3)).astype(BF)


def image_body(ids, e0, e1, e2, e3, image, gain, g1, layer, both, dgain):
    e = sum_four(e0, e1, e2, e3)
    back, dg = norm_back(image[...].astype(F32), gain[...], e)
    both[0] = (g1[...] + back).astype(BF)
    both[1] = layer[...]
    dgain[...] = jnp.concatenate([dg[128 * m : 128 * m + 128].reshape(1, 128) for m in range(8)])


def text_body(ids, recv, wck, wcv, own, other):
    acc = recv[0, 64:192].astype(F32)
    for j in range(1, 8):
        acc += recv[j, 64:192].astype(F32)
    d = acc.astype(BF)
    tp = dot(d[:, 0:128], wck[...], 0, 1) + dot(d[:, 128:256], wcv[...], 0, 1)
    parts = [fold(tp[8 * n : 8 * n + 8]) for n in range(16)]
    rows = [jnp.concatenate([parts[n], parts[8 + n]], axis=0).astype(BF) for n in range(8)]
    all_rows = jnp.concatenate(rows, axis=0).reshape(8, 128, 128)
    for n in range(8):
        x = lax.rem(lax.div(ids[1], 2) + 4 - n // 2, 4)
        core = lax.rem(ids[1] + n % 2, 2)

        @pl.when(core == 0)
        def _():
            own[x] = all_rows[n]

        @pl.when(core == 1)
        def _():
            other[x] = all_rows[n]


def text_pair_body(ids, p0, p1, p2, p3, mine, theirs):
    total = sum_four(p0, p1, p2, p3)
    odd = lax.rem(ids[0], 2) == 1
    mine[...] = jnp.where(odd, total[64:128], total[0:64])
    theirs[...] = jnp.where(odd, total[0:64], total[64:128]).astype(BF)


def weight_grad_body(
    ids,
    a0,
    a1,
    a2,
    a3,
    others,
    recv,
    self_cols,
    g1,
    text,
    dqkv,
    out,
    s1,
    s2,
    sg,
):
    for k, a in enumerate((a0, a1, a2, a3)):
        for to, v in ((slot(ids, k), a[...]), (slot(ids, 4 + k), others[k])):
            s2[to] = v[:, 0:1024]
            sg[to] = v[:, 1024:2048]
            s1[to] = v[:, 2048:3072]
    flat = lambda v: v.reshape(512, v.shape[-1])
    cross, dcq = flat(recv[:, 0:64, 0:128]), flat(recv[:, 0:64, 128:256])
    blocks = lambda v: v.astype(BF).reshape(16, 64, v.shape[-1])
    out[:, :, 0:384] = blocks(dot(flat(s1[...]), flat(dqkv[...]), 0, 0))
    out[:, :, 384:512] = blocks(dot(flat(s2[...]), dcq, 0, 0))
    acc = recv[0, 64:192].astype(F32)
    for j in range(1, 8):
        acc += recv[j, 64:192].astype(F32)
    d = acc.astype(BF)
    out[:, :, 512:640] = blocks(dot(text[0], d[:, 0:128], 0, 1))
    out[:, :, 640:768] = blocks(dot(text[0], d[:, 128:256], 0, 1))
    dao = dot(flat(self_cols[...]), flat(g1[...]), 0, 0)
    dco = dot(cross, flat(sg[...]), 0, 0)
    for b in range(16):
        rows = slice(8 * b, 8 * b + 8)
        out[b, :, 768:896] = fold(dao[rows]).astype(BF)
        out[b, :, 896:1024] = fold(dco[rows]).astype(BF)


def sum_body(ids, got, first, second):
    for rows, out in ((slice(0, 32), first), (slice(32, 64), second)):
        acc = got[0, rows].astype(F32)
        for b in range(1, 16):
            acc += got[b, rows].astype(F32)
        out[...] = acc.astype(BF)


def text_sum_body(ids, mine, got, dgain23, dgain1, out):
    out[0:64] = (mine[...] + got[...].astype(F32)).astype(BF)
    out[64:80] = dgain23[...].astype(BF)
    out[80:96] = jnp.concatenate([dgain1[...], jnp.zeros((8, 128), F32)]).astype(BF)


def text_place_body(ids, own, other, out, dgain, gains):
    for s, ref in enumerate((own, other)):
        for k in range(4):
            t = slot(ids, 4 * s + k)
            for n in range(16):
                place = 8 * band_slot(ids, n) + t
                v = ref[k, n // 4, n % 4].astype(F32)
                out[pl.ds(pl.multiple_of(8 * place, 8), 8)] = jnp.concatenate(
                    [v[8 * m : 8 * m + 8] for m in range(8)], axis=1
                )
                gains[place] = v[64:96]
    acc = gains[0]
    for n in range(1, 128):
        acc += gains[n]
    dgain[...] = acc


def place_body(ids, parts, gimg, layer):
    for t in range(8):
        gimg[t] = parts[t, 0].astype(F32)
        layer[t] = parts[t, 1]


def place_weights_body(ids, a0, a1, a2, a3, b0, b1, b2, b3, o0, o1, o2, o3, o4, o5, o6, o7):
    for n in range(16):
        b = band_slot(ids, n)
        ky, kz = n // 4, n % 4
        halves = ((a0, a1, a2, a3)[ky][kz], (b0, b1, b2, b3)[kz][ky])
        for h, half in enumerate(halves):
            block = half.astype(F32)
            rows = pl.ds(pl.multiple_of(64 * b + 32 * h, 32), 32)
            for c, o in enumerate((o0, o1, o2, o3, o4, o5)):
                o[rows] = block[:, 128 * c : 128 * c + 128]
            rows = pl.ds(pl.multiple_of(8 * b, 8), 8)
            for c, o in enumerate((o6, o7)):
                cols = block[:, 768 + 128 * c : 896 + 128 * c]
                for m in range(4):
                    lanes = slice(128 * (4 * h + m), 128 * (4 * h + m) + 128)
                    o[rows, lanes] = cols[8 * m : 8 * m + 8]


def after(v, *deps):
    return lax.optimization_barrier((v, *deps))[0]


same_core = [[0, 2, 4, 6], [1, 3, 5, 7]]


def swap_x(v):
    return lax.all_to_all(v, "tp", 0, 0, axis_index_groups=same_core)


def shifts(v):
    return [v] + [x_shift(v, k) for k in (1, 2, 3)]


def gather_parts(v):
    own = shifts(v)
    return own, core_swap(jnp.stack(own))


def add_cores(own, other):
    got = core_swap(other)
    return [(own[k].astype(F32) + got[k].astype(F32)).astype(BF) for k in range(4)]


def scatter_x(both):
    return [both[0]] + [x_shift(both[k], -k) for k in (1, 2, 3)]


def local(
    image_in,
    text_in,
    text_len,
    cotangent,
    gain_one,
    w_query,
    w_key,
    w_value,
    w_attn_out,
    gain_two,
    w_cross_q,
    w_cross_k,
    w_cross_v,
    w_cross_out,
    gain_three,
    w_hidden,
    w_back,
):
    ids = jnp.stack([lax.axis_index("band"), lax.axis_index("tp")])
    row = lambda g: g.reshape(1, 1024)
    chunk, four = ((64, 1024), BF), ((4, 64, 1024), BF)

    send, image_c = kernel_call(
        qkv_body,
        [((16, 64, 512), BF), chunk],
        [ids, image_in, row(gain_one), w_query, w_key, w_value],
        scratch=[pltpu.VMEM((512, 1024), BF)],
        mib=60,
    )
    got = lax.all_to_all(send, "band", 0, 0)

    (wbuf,) = kernel_call(
        prep_body,
        [((128, 2304), BF)],
        [ids, of_item(after(text_in, send)), w_cross_q, w_cross_k, w_cross_v, w_cross_out],
        mib=60,
    )
    near = [wbuf, x_shift(wbuf, 1), x_shift(wbuf, 3)]
    far = [x_shift(near[1][:, :1024], 1), x_shift(near[2][:, 1024:], 3)]
    w_own = [near[0], near[1], *far, near[2]]
    w_all = w_own + [core_swap(v) for v in w_own]

    got = after(got, wbuf)
    self_cols, probs, own, other = kernel_call(
        attend_body,
        [((8, 64, 128), BF), ((8, 128, 1024), BF), four, four],
        [ids, got, w_attn_out],
        us=10,
    )
    fwd = add_cores(own, other)
    cot_send = after(cotangent, fwd[1])
    fwd = [after(v, *far) for v in fwd]
    parts = scatter_x(fwd)

    same = [[2 * j + p for j in range(8)] for p in (0, 1)]
    cot_all = lax.all_to_all(cot_send, "band", 0, 0, axis_index_groups=same)
    after_self, a2, cq, cprobs, cross, after_cross, a3 = kernel_call(
        middle_body,
        [
            ((64, 1024), F32),
            chunk,
            ((8, 64, 128), BF),
            ((8, 128, 128), BF),
            ((8, 64, 128), BF),
            ((64, 1024), F32),
            chunk,
        ],
        [ids, text_len, *parts, row(gain_two), row(gain_three), *w_all],
        smem=2,
        mib=60,
        us=10,
    )

    image_c = to_item(after(image_c, fwd[1]))
    a3_own, a3_other = gather_parts(after(a3, image_c))
    dact = dot(after(cot_all, a3).reshape(512, 1024), w_back, 1, 1)
    hid, dpre, da_own, da_other, a3_all = kernel_call(
        hidden_body,
        [((512, 512), BF), ((8, 64, 512), BF), four, four, ((8, 64, 1024), BF)],
        [ids, *a3_own, a3_other, dact, w_hidden],
    )
    both = (da_own.astype(F32) + core_swap(da_other).astype(F32)).astype(BF)
    da3 = swap_x(both)
    quarter = ((4, 64, 1024), BF)
    own, other, dw_back, dw_hidden = kernel_call(
        hidden_grad_body,
        [four, four, ((512, 1024), F32), ((1024, 512), F32)],
        [ids, after(hid, both), dpre, a3_all, cot_all, w_back],
        scratch=[pltpu.VMEM((8, 64, 1024), BF)],
        mib=60,
        us=10,
    )
    dw_back, dw_hidden = lax.psum((dw_back, dw_hidden), "band")
    a2g2, g1_low, g1, cols, dgain23 = kernel_call(
        middle_back_body,
        [((64, 3072), BF), chunk, ((64, 1024), F32), ((8, 192, 256), BF), ((16, 128), F32)],
        [ids, da3, of_tp(after(cot_all, own)), after_cross, after_self, cq, cprobs, cross]
        + [image_c, row(gain_one), row(gain_two), row(gain_three)]
        + w_all,
        scratch=[pltpu.VMEM((64, 1024), F32)],
        mib=60,
    )

    out_both = add_cores(after(own, g1_low), other)
    g1_own = shifts(g1_low)
    g1_other = core_swap(jnp.stack([after(v, *out_both) for v in g1_own]))
    out_parts = scatter_x([after(v, g1_other) for v in out_both])
    (layer_c,) = kernel_call(layer_body, [chunk], [ids, *out_parts, after_cross])
    dq, kv_own, kv_other, g1_all = kernel_call(
        attend_back_body,
        [((8, 64, 128), BF), ((8, 64, 256), F32), ((8, 64, 256), BF), ((8, 64, 1024), BF)],
        [ids, got, probs, w_attn_out, *g1_own, g1_other],
        scratch=[pltpu.VMEM((1024, 128), F32)] * 2 + [pltpu.VMEM((8, 64, 128), BF)],
        mib=60,
    )
    mid_own = shifts(after(a2g2, kv_other))
    kv_got = lax.ppermute(kv_other, "band", [(b, b ^ 1) for b in range(16)])
    recv = lax.all_to_all(after(cols, *g1_own[1:]), "tp", 0, 0)
    dqkv, own, other = kernel_call(
        first_body,
        [((8, 64, 384), BF), four, four],
        [ids, dq, kv_own, kv_got, after(w_query, recv), w_key, w_value],
    )
    both = add_cores(own, other)
    e1 = scatter_x(both)
    mid_other = core_swap(jnp.stack([after(v, dqkv) for v in mid_own]))
    (grads,) = kernel_call(
        weight_grad_body,
        [((16, 64, 1024), BF)],
        [ids, *mid_own, mid_other, recv, self_cols, g1_all, of_item(text_in)]
        + [after(dqkv, both[1])],
        scratch=[pltpu.VMEM((8, 64, 1024), BF)] * 3,
        mib=60,
    )
    grads_got = lax.all_to_all(grads, "band", 0, 0)
    tile = ((4, 128, 128), BF)
    t_own, t_other = kernel_call(
        text_body, [tile, tile], [ids, after(recv, grads), w_cross_k, w_cross_v], mib=60
    )
    last, dgain1 = kernel_call(
        image_body,
        [((2, 64, 1024), BF), ((8, 128), F32)],
        [ids, *e1, image_c, row(gain_one), after(g1, t_own), layer_c],
        mib=60,
    )
    moved = to_band(last)

    t_parts = scatter_x(add_cores(t_own, t_other))
    t_mine, t_theirs = kernel_call(
        text_pair_body, [((64, 128), F32), ((64, 128), BF)], [ids, after(t_parts[0], grads_got), *t_parts[1:]]
    )
    grads_got = after(grads_got, t_theirs)
    half = ((32, 1024), BF)
    ga0, gb0 = kernel_call(sum_body, [half, half], [ids, grads_got], mib=60)
    ga = jnp.stack([ga0] + [z_shift(ga0, k) for k in (1, 2, 3)])
    gb = jnp.stack([gb0] + [y_shift(gb0, k) for k in (1, 2, 3)])
    t_got = lax.ppermute(after(t_theirs, ga0), "band", [(b, b ^ 1) for b in range(16)])
    (tsum,) = kernel_call(
        text_sum_body, [((96, 128), BF)], [ids, t_mine, t_got, dgain23, dgain1]
    )

    tz = jnp.stack([tsum] + [z_shift(tsum, k) for k in (1, 2, 3)])
    ty = jnp.stack([tz] + [y_shift(tz, k) for k in (1, 2, 3)])
    ga = [ga] + [y_shift(ga, k) for k in (1, 2, 3)]
    gb = [gb] + [z_shift(gb, k) for k in (1, 2, 3)]
    last_all = lax.all_gather(after(moved, t_theirs), "tp", axis=0)
    dw_back, dw_hidden = kernel_call(
        copy_body, [((512, 1024), F32), ((1024, 512), F32)], [ids, dw_back, dw_hidden], mib=60
    )
    gimg, layer_out = kernel_call(
        place_body,
        [((8, 64, 1024), F32), ((8, 64, 1024), BF)],
        [ids, last_all],
        mib=60,
    )
    tall = jnp.stack([after(v, *ga[1:], *gb[1:], gimg, dw_back) for v in shifts(ty)])
    tall = [tall, core_swap(tall)]
    grad_text, dgains = kernel_call(
        text_place_body,
        [((1024, 1024), F32), ((32, 128), F32)],
        [ids, *tall],
        scratch=[pltpu.VMEM((128, 32, 128), F32)],
    )
    dw_query, dw_key, dw_value, dw_cross_q, dw_cross_k, dw_cross_v, dw_attn_out, dw_cross_out = (
        kernel_call(
            place_weights_body,
            [((1024, 128), F32)] * 6 + [((128, 1024), F32)] * 2,
            [ids, after(ga[0], gimg, dw_back), *ga[1:], *gb],
        )
    )
    return (
        layer_out,
        gimg,
        grad_text.reshape(8, 128, 1024),
        dgains[16:24].reshape(1024),
        dw_query,
        dw_key,
        dw_value,
        dw_attn_out,
        dgains[0:8].reshape(1024),
        dw_cross_q,
        dw_cross_k,
        dw_cross_v,
        dw_cross_out,
        dgains[8:16].reshape(1024),
        dw_hidden,
        dw_back,
    )


def solution(mesh):
    rows, cols, heads = P(None, "band", None), P(None, "tp"), P("tp", None)
    in_specs = (
        rows, P(), P(), rows, P(), cols, cols, cols, heads, P(), cols, cols, cols, heads, P(), cols, heads,
    )
    out_specs = (
        rows, rows, P(), P(), cols, cols, cols, heads, P(), cols, cols, cols, heads, P(), cols, heads,
    )
    return jax.shard_map(local, mesh=mesh, in_specs=in_specs, out_specs=out_specs, check_vma=False)
```

```python
import jax
import jax.numpy as jnp
from jax import lax
from jax.experimental import pallas as pl
from jax.experimental.pallas import tpu as pltpu
from jax.sharding import PartitionSpec as P

HD = 64
norm_eps = 1e-05
mask_fill = -1000000000.0
BF = jnp.bfloat16
F32 = jnp.float32


def dot(a, b, ca, cb):
    return lax.dot_general(a, b, (((ca,), (cb,)), ((), ())), preferred_element_type=F32)


def norm_parts(rows):
    centred = rows - jnp.mean(rows, axis=-1, keepdims=True)
    inv = lax.rsqrt(jnp.mean(centred * centred, axis=-1, keepdims=True) + norm_eps)
    return centred * inv, inv


def norm_back(rows, gain, grad):
    xh, inv = norm_parts(rows)
    eg = grad * gain
    back = inv * (
        eg
        - jnp.mean(eg, axis=-1, keepdims=True)
        - xh * jnp.mean(eg * xh, axis=-1, keepdims=True)
    )
    return back, jnp.sum((grad * xh).reshape(-1, rows.shape[-1]), axis=0)


def x_shift(v, k):
    return lax.ppermute(v, "tp", [(t, (t + 2 * k) % 8) for t in range(8)])


def core_swap(v):
    return lax.ppermute(v, "tp", [(t, t ^ 1) for t in range(8)])


def z_shift(v, k):
    return lax.ppermute(v, "band", [(b, b // 4 * 4 + (b + k) % 4) for b in range(16)])


def y_shift(v, k):
    return lax.ppermute(v, "band", [(b, (b + 4 * k) % 16) for b in range(16)])


def gather_band(v):
    rows = jnp.stack([v] + [z_shift(v, k) for k in (1, 2, 3)])
    return jnp.stack([rows] + [y_shift(rows, k) for k in (1, 2, 3)])


def to_item(v):
    perm = [(c * 8 + i, (2 * i + c % 2) * 8 + c // 2) for c in range(16) for i in range(8)]
    return lax.ppermute(v, ("band", "tp"), perm)


def to_band(v):
    perm = [((2 * i + c % 2) * 8 + c // 2, c * 8 + i) for c in range(16) for i in range(8)]
    return lax.ppermute(v, ("band", "tp"), perm)


def kernel_call(body, outs, args, smem=1, scratch=(), mib=40, us=0):
    def whole(shape):
        return pl.BlockSpec(
            shape, lambda *_: (0,) * len(shape), pipeline_mode=pl.Buffered(buffer_count=1)
        )

    def block(arg):
        if not isinstance(arg, tuple):
            return whole(arg.shape)
        array, first, place = arg
        rest = array.shape[1:]
        return pl.BlockSpec(
            (first, *rest),
            lambda _, *scalars: (place(*scalars), *(0 for _ in rest)),
            pipeline_mode=pl.Buffered(buffer_count=1),
        )

    arrays = [a[0] if isinstance(a, tuple) else a for a in args]
    return pl.pallas_call(
        body,
        out_shape=[jax.ShapeDtypeStruct(s, d) for s, d in outs],
        grid_spec=pltpu.PrefetchScalarGridSpec(
            num_scalar_prefetch=smem,
            grid=(1,),
            in_specs=[block(a) for a in args[smem:]],
            out_specs=[whole(s) for s, _ in outs],
            scratch_shapes=list(scratch),
        ),
        compiler_params=pltpu.CompilerParams(vmem_limit_bytes=mib * 2**20),
        cost_estimate=pl.CostEstimate(
            flops=1, bytes_accessed=1 + us * 3700000, transcendentals=0
        ),
    )(*arrays)


def of_item(v):
    return (v, 1, lambda ids, *_: lax.div(ids[0], 2))


def of_tp(v):
    return (v, 1, lambda ids, *_: ids[1])


def slot(ids, s):
    t = ids[1]
    x = lax.rem(lax.div(t, 2) + 4 - s % 4, 4)
    core = lax.rem(t + s // 4, 2)
    return 2 * x + core


def side(ids, s, x):
    return 2 * x + lax.rem(ids[1] + s, 2)


def band_slot(ids, n):
    y, z = lax.div(ids[0], 4), lax.rem(ids[0], 4)
    return 4 * lax.rem(y + 4 - n // 4, 4) + lax.rem(z + 4 - n % 4, 4)


def head_rows(v):
    first = lax.broadcasted_iota(jnp.int32, v.shape, 1) < 64
    zero = jnp.zeros_like(v)
    return jnp.concatenate([jnp.where(first, v, zero), jnp.where(first, zero, v)], axis=0)


def head_cols(v):
    r = v.shape[0] // 2
    first = lax.broadcasted_iota(jnp.int32, (r, 128), 1) < 64
    return jnp.where(first, v[:r], v[r:])


def soft(s):
    e = jnp.exp(s - jnp.max(s, axis=-1, keepdims=True))
    return (e / jnp.sum(e, axis=-1, keepdims=True)).astype(BF)


def soft_back(p, dp):
    pf = p.astype(F32)
    return (pf * (dp - jnp.sum(dp * pf, axis=-1, keepdims=True))).astype(BF)


def sum_four(e0, e1, e2, e3):
    return (e0[...].astype(F32) + e2[...].astype(F32)) + (
        e1[...].astype(F32) + e3[...].astype(F32)
    )


def fold(v):
    return jnp.concatenate([v[:, 128 * m : 128 * m + 128] for m in range(8)], axis=0)


def qkv_body(ids, image, gain, wq, wk, wv, send, own, a1):
    own[...] = image[ids[1]]
    for i in range(8):
        xh, _ = norm_parts(image[i].astype(F32))
        a1[i * 64 : i * 64 + 64] = (xh * gain[...]).astype(BF)
    w = jnp.concatenate([wq[...], wk[...], wv[...]], axis=1)
    qkv = dot(a1[...], w, 1, 0).astype(BF).reshape(8, 64, 384)
    cols = pl.ds(pl.multiple_of(ids[1] * 128, 128), 128)
    for i in range(8):
        part = image[i, :, cols]
        for p in (0, 1):
            send[2 * i + p, :, 0:384] = qkv[i]
            send[2 * i + p, :, 384:512] = part


def prep_body(ids, text, wcq, wck, wcv, wco, buf):
    mine = text[0]
    buf[:, 0:1024] = jnp.transpose(wcq[...].astype(F32)).astype(BF)
    buf[:, 1024:2048] = wco[...]
    buf[:, 2048:2176] = dot(wck[...], mine, 0, 1).astype(BF)
    buf[:, 2176:2304] = dot(wcv[...], mine, 0, 1).astype(BF)


def attend_body(ids, got, wo, cols, probs, own, other):
    par = lax.rem(ids[0], 2)
    for j in range(8):
        n = 128 * (j + 1)
        q = head_rows(got[2 * j + par, :, 0:128])
        k = got[0 : 2 * j + 2, :, 128:256].reshape(n, 128)
        v = got[0 : 2 * j + 2, :, 256:384].reshape(n, 128)
        s = dot(q, k, 1, 1) * 0.125
        row = lax.broadcasted_iota(jnp.int32, (128, n), 0) % 64 + (128 * j + 64 * par)
        s = jnp.where(lax.broadcasted_iota(jnp.int32, (128, n), 1) <= row, s, mask_fill)
        p = soft(s)
        probs[j, :, 0:n] = p
        cols[j] = head_cols(dot(p, v, 1, 0)).astype(BF)
    mine = pl.ds(pl.multiple_of(ids[1] * 128, 128), 128)
    for ref, first in ((other, 4), (own, 0)):
        c = jnp.concatenate([cols[slot(ids, first + k)] for k in range(4)], axis=0)
        ref[...] = dot(c, wo[...], 1, 0).astype(BF).reshape(4, 64, 1024)
        part = dot(c, wo[:, mine], 1, 0)
        for k in range(4):
            res = got[2 * slot(ids, first + k) + par, :, 384:512].astype(F32)
            ref[k, :, mine] = (part[64 * k : 64 * k + 64] + res).astype(BF)


def attend_back_body(
    ids, got, probs, wo, a0, a1, a2, a3, others, dq, kv_own, kv_other, g1, dk, dv, dheads
):
    par = lax.rem(ids[0], 2)
    for k, a in enumerate((a0, a1, a2, a3)):
        g1[slot(ids, k)] = a[...]
        g1[slot(ids, 4 + k)] = others[k]
    dheads[...] = dot(g1[...].reshape(512, 1024), wo[...], 1, 1).astype(BF).reshape(8, 64, 128)
    dk[...] = jnp.zeros_like(dk)
    dv[...] = jnp.zeros_like(dv)
    for j in range(8):
        n = 128 * (j + 1)
        q = head_rows(got[2 * j + par, :, 0:128])
        k = got[0 : 2 * j + 2, :, 128:256].reshape(n, 128)
        v = got[0 : 2 * j + 2, :, 256:384].reshape(n, 128)
        g = head_rows(dheads[j])
        p = probs[j, :, 0:n]
        ds = soft_back(p, dot(g, v, 1, 1))
        dv[0:n] += dot(p, g, 0, 0)
        dk[0:n] += dot(ds, q, 0, 0)
        dq[j] = (head_cols(dot(ds, k, 1, 0)) * 0.125).astype(BF)
    for j in range(8):
        own = pl.ds(pl.multiple_of(128 * j + 64 * par, 64), 64)
        other = pl.ds(pl.multiple_of(128 * j + 64 - 64 * par, 64), 64)
        kv_own[j, :, 0:128] = dk[own] * 0.125
        kv_own[j, :, 128:256] = dv[own]
        kv_other[j, :, 0:128] = (dk[other] * 0.125).astype(BF)
        kv_other[j, :, 128:256] = dv[other].astype(BF)


def split_weights(refs):
    halves = []
    for first in (0, 5):
        a, b, q, o, c = refs[first : first + 5]
        cut = [(r.at[:, 0:1024], r.at[:, 1024:2304]) for r in (a, b, c)]
        halves += [cut[0], cut[1], (q, o), cut[2]]
    return [h[0] for h in halves], [h[1] for h in halves]


def middle_body(ids, tlen, e0, e1, e2, e3, gain2, gain3, *refs):
    (wq, wo), outs = split_weights(refs[:10]), refs[10:]
    after_self, a2, cq, probs, cross, after_cross, a3 = outs
    acc = sum_four(e0, e1, e2, e3)
    after_self[...] = acc
    xh, _ = norm_parts(acc)
    a2[...] = (xh * gain2[...]).astype(BF)
    live = lax.broadcasted_iota(jnp.int32, (128, 128), 1) < tlen[lax.div(ids[0], 2)]
    for s in range(8):
        cqs = dot(a2[...], wq[s][...], 1, 1).astype(BF)
        cq[s] = cqs
        sc = dot(head_rows(cqs), wo[s][:, 1024:1152], 1, 0) * 0.125
        p = soft(jnp.where(live, sc, mask_fill))
        probs[s] = p
        cross[s] = head_cols(dot(p, wo[s][:, 1152:1280], 1, 1)).astype(BF)
    acc = after_self[...]
    for s in range(8):
        acc += dot(cross[s], wo[s][:, 0:1024], 1, 0)
    after_cross[...] = acc
    xh, _ = norm_parts(acc)
    a3[...] = (xh * gain3[...]).astype(BF)


def middle_back_body(ids, parts, cot, after_cross, after_self, cq, probs, cross, image, gain1, gain2, gain3, *refs):
    (wq, wo), (both, g1_low, g1, cols, dgain, g2) = split_weights(refs[:10]), refs[10:]
    e = sum_four(*(parts.at[x] for x in range(4)))
    back, dg3 = norm_back(after_cross[...], gain3[...], e)
    g2[...] = cot[0].astype(F32) + back
    g2l = g2[...].astype(BF)
    both[:, 1024:2048] = g2l
    xh, _ = norm_parts(image[...].astype(F32))
    both[:, 2048:3072] = (xh * gain1[...]).astype(BF)
    da2 = jnp.zeros((64, 1024), F32)
    for s in range(8):
        dc = head_rows(dot(g2l, wo[s][:, 0:1024], 1, 1).astype(BF))
        p = probs[s]
        ds = soft_back(p, dot(dc, wo[s][:, 1152:1280], 1, 0))
        dq = (head_cols(dot(ds, wo[s][:, 1024:1152], 1, 1)) * 0.125).astype(BF)
        dk = dot(head_rows(cq[s]), ds, 0, 0) * 0.125
        dv = dot(dc, p, 0, 0)
        to = slot(ids, s)
        cols[to, 0:64, 0:128] = cross[s]
        cols[to, 0:64, 128:256] = dq
        cols[to, 64:192, 0:128] = dk.astype(BF)
        cols[to, 64:192, 128:256] = dv.astype(BF)
        da2 += dot(dq, wq[s][...], 1, 0)
    v = after_self[...]
    xh, _ = norm_parts(v)
    both[:, 0:1024] = (xh * gain2[...]).astype(BF)
    back, dg2 = norm_back(v, gain2[...], da2)
    g1[...] = g2[...] + back
    g1l = g1[...].astype(BF)
    g1_low[...] = g1l
    dgain[0:8] = jnp.concatenate([dg2[128 * m : 128 * m + 128].reshape(1, 128) for m in range(8)])
    dgain[8:16] = jnp.concatenate([dg3[128 * m : 128 * m + 128].reshape(1, 128) for m in range(8)])


def hidden_body(ids, a0, a1, a2, a3, others, dact, wh, hid, dpre, da_own, da_other, a3_all):
    for k, a in enumerate((a0, a1, a2, a3)):
        a3_all[slot(ids, k)] = a[...]
        a3_all[slot(ids, 4 + k)] = others[k]
    for r in range(4):
        rows = slice(128 * r, 128 * r + 128)
        u = dot(a3_all[2 * r : 2 * r + 2].reshape(128, 1024), wh[...], 1, 0)
        th = jnp.tanh(0.7978845608028654 * (u + 0.044715 * u * u * u))
        hid[rows] = (0.5 * u * (1.0 + th)).astype(BF)
        slope = 0.5 * (1.0 + th) + 0.5 * u * (1.0 - th * th) * (
            0.7978845608028654 * (1.0 + 0.134145 * u * u)
        )
        dpre[2 * r : 2 * r + 2] = (dact[rows] * slope).astype(BF).reshape(2, 64, 512)
    for ref, s in ((da_other, 1), (da_own, 0)):
        d = jnp.concatenate([dpre[side(ids, s, x)] for x in range(4)], axis=0)
        ref[...] = dot(d, wh[...], 1, 1).astype(BF).reshape(4, 64, 1024)


def hidden_grad_body(ids, hid, dpre, a3_all, cot, wb, own, other, dwb, dwh, part):
    h = hid[...]
    part[...] = dot(h, wb[...], 1, 0).astype(BF).reshape(8, 64, 1024)
    for k in range(4):
        own[k] = part[slot(ids, k)]
        other[k] = part[slot(ids, 4 + k)]
    dwb[...] = dot(h, cot[...].reshape(512, 1024), 0, 0)
    dwh[...] = dot(a3_all[...].reshape(512, 1024), dpre[...].reshape(512, 512), 0, 0)


def first_body(ids, dq, kv_own, kv_got, wq, wk, wv, dqkv, own, other):
    for j in range(8):
        dqkv[j, :, 0:128] = dq[j]
        dqkv[j, :, 128:384] = (kv_own[j] + kv_got[j].astype(F32)).astype(BF)
    w = jnp.concatenate([wq[...], wk[...], wv[...]], axis=1)
    for ref, first in ((other, 4), (own, 0)):
        d = jnp.concatenate([dqkv[slot(ids, first + k)] for k in range(4)], axis=0)
        ref[...] = dot(d, w, 1, 1).astype(BF).reshape(4, 64, 1024)


def copy_body(ids, dwb, dwh, out_b, out_h):
    out_b[...] = dwb[...]
    out_h[...] = dwh[...]


def layer_body(ids, p0, p1, p2, p3, after_cross, out):
    out[...] = (after_cross[...] + sum_four(p0, p1, p2, p3)).astype(BF)


def image_body(ids, e0, e1, e2, e3, image, gain, g1, layer, both, dgain):
    e = sum_four(e0, e1, e2, e3)
    back, dg = norm_back(image[...].astype(F32), gain[...], e)
    both[0] = (g1[...] + back).astype(BF)
    both[1] = layer[...]
    dgain[...] = jnp.concatenate([dg[128 * m : 128 * m + 128].reshape(1, 128) for m in range(8)])


def text_body(ids, recv, wck, wcv, own, other):
    acc = recv[0, 64:192].astype(F32)
    for j in range(1, 8):
        acc += recv[j, 64:192].astype(F32)
    d = acc.astype(BF)
    tp = dot(d[:, 0:128], wck[...], 0, 1) + dot(d[:, 128:256], wcv[...], 0, 1)
    parts = [fold(tp[8 * n : 8 * n + 8]) for n in range(16)]
    rows = [jnp.concatenate([parts[n], parts[8 + n]], axis=0).astype(BF) for n in range(8)]
    all_rows = jnp.concatenate(rows, axis=0).reshape(8, 128, 128)
    for n in range(8):
        x = lax.rem(lax.div(ids[1], 2) + 4 - n // 2, 4)
        core = lax.rem(ids[1] + n % 2, 2)

        @pl.when(core == 0)
        def _():
            own[x] = all_rows[n]

        @pl.when(core == 1)
        def _():
            other[x] = all_rows[n]


def text_pair_body(ids, p0, p1, p2, p3, mine, theirs):
    total = sum_four(p0, p1, p2, p3)
    odd = lax.rem(ids[0], 2) == 1
    mine[...] = jnp.where(odd, total[64:128], total[0:64])
    theirs[...] = jnp.where(odd, total[0:64], total[64:128]).astype(BF)


def weight_grad_body(
    ids,
    a0,
    a1,
    a2,
    a3,
    others,
    recv,
    self_cols,
    g1,
    text,
    dqkv,
    out,
    s1,
    s2,
    sg,
):
    for k, a in enumerate((a0, a1, a2, a3)):
        for to, v in ((slot(ids, k), a[...]), (slot(ids, 4 + k), others[k])):
            s2[to] = v[:, 0:1024]
            sg[to] = v[:, 1024:2048]
            s1[to] = v[:, 2048:3072]
    flat = lambda v: v.reshape(512, v.shape[-1])
    cross, dcq = flat(recv[:, 0:64, 0:128]), flat(recv[:, 0:64, 128:256])
    blocks = lambda v: v.astype(BF).reshape(16, 64, v.shape[-1])
    out[:, :, 0:384] = blocks(dot(flat(s1[...]), flat(dqkv[...]), 0, 0))
    out[:, :, 384:512] = blocks(dot(flat(s2[...]), dcq, 0, 0))
    acc = recv[0, 64:192].astype(F32)
    for j in range(1, 8):
        acc += recv[j, 64:192].astype(F32)
    d = acc.astype(BF)
    out[:, :, 512:640] = blocks(dot(text[0], d[:, 0:128], 0, 1))
    out[:, :, 640:768] = blocks(dot(text[0], d[:, 128:256], 0, 1))
    dao = dot(flat(self_cols[...]), flat(g1[...]), 0, 0)
    dco = dot(cross, flat(sg[...]), 0, 0)
    for b in range(16):
        rows = slice(8 * b, 8 * b + 8)
        out[b, :, 768:896] = fold(dao[rows]).astype(BF)
        out[b, :, 896:1024] = fold(dco[rows]).astype(BF)


def sum_body(ids, got, out):
    acc = got[0].astype(F32)
    for b in range(1, 16):
        acc += got[b].astype(F32)
    out[...] = acc.astype(BF)


def text_sum_body(ids, mine, got, dgain23, out):
    out[0:64] = (mine[...] + got[...].astype(F32)).astype(BF)
    out[64:80] = dgain23[...].astype(BF)


def text_place_body(ids, parts, out, dgain):
    acc = jnp.zeros((16, 128), F32)
    for n in range(128):
        v = parts[80 * n : 80 * n + 80].astype(F32)
        out[8 * n : 8 * n + 8] = jnp.concatenate(
            [v[8 * m : 8 * m + 8] for m in range(8)], axis=1
        )
        acc += v[64:80]
    dgain[...] = acc


def place_body(ids, parts, gimg, layer):
    for t in range(8):
        gimg[t] = parts[t, 0].astype(F32)
        layer[t] = parts[t, 1]


def place_weights_body(ids, p0, p1, p2, p3, o0, o1, o2, o3, o4, o5, o6, o7):
    for n in range(16):
        b = band_slot(ids, n)
        block = (p0, p1, p2, p3)[n // 4][n % 4].astype(F32)
        rows = pl.ds(pl.multiple_of(64 * b, 64), 64)
        for c, o in enumerate((o0, o1, o2, o3, o4, o5)):
            o[rows] = block[:, 128 * c : 128 * c + 128]
        rows = pl.ds(pl.multiple_of(8 * b, 8), 8)
        for c, o in enumerate((o6, o7)):
            cols = block[:, 768 + 128 * c : 896 + 128 * c]
            for m in range(8):
                o[rows, 128 * m : 128 * m + 128] = cols[8 * m : 8 * m + 8]


def after(v, *deps):
    return lax.optimization_barrier((v, *deps))[0]


same_core = [[0, 2, 4, 6], [1, 3, 5, 7]]


def swap_x(v):
    return lax.all_to_all(v, "tp", 0, 0, axis_index_groups=same_core)


def sum_four_places(v, move):
    return (v + move(v, 2)) + (move(v, 1) + move(v, 3))


def shifts(v):
    return [v] + [x_shift(v, k) for k in (1, 2, 3)]


def gather_parts(v):
    own = shifts(v)
    return own, core_swap(jnp.stack(own))


def add_cores(own, other):
    got = core_swap(other)
    return [(own[k].astype(F32) + got[k].astype(F32)).astype(BF) for k in range(4)]


def scatter_x(both):
    return [both[0]] + [x_shift(both[k], -k) for k in (1, 2, 3)]


def local(
    image_in,
    text_in,
    text_len,
    cotangent,
    gain_one,
    w_query,
    w_key,
    w_value,
    w_attn_out,
    gain_two,
    w_cross_q,
    w_cross_k,
    w_cross_v,
    w_cross_out,
    gain_three,
    w_hidden,
    w_back,
):
    ids = jnp.stack([lax.axis_index("band"), lax.axis_index("tp")])
    row = lambda g: g.reshape(1, 1024)
    chunk, four = ((64, 1024), BF), ((4, 64, 1024), BF)

    send, image_c = kernel_call(
        qkv_body,
        [((16, 64, 512), BF), chunk],
        [ids, image_in, row(gain_one), w_query, w_key, w_value],
        scratch=[pltpu.VMEM((512, 1024), BF)],
        mib=60,
    )
    got = lax.all_to_all(send, "band", 0, 0)

    (wbuf,) = kernel_call(
        prep_body,
        [((128, 2304), BF)],
        [ids, of_item(after(text_in, send)), w_cross_q, w_cross_k, w_cross_v, w_cross_out],
        mib=60,
    )
    near = [wbuf, x_shift(wbuf, 1), x_shift(wbuf, 3)]
    far = [x_shift(near[1][:, :1024], 1), x_shift(near[2][:, 1024:], 3)]
    w_own = [near[0], near[1], *far, near[2]]
    w_all = w_own + [core_swap(v) for v in w_own]

    got = after(got, wbuf)
    self_cols, probs, own, other = kernel_call(
        attend_body,
        [((8, 64, 128), BF), ((8, 128, 1024), BF), four, four],
        [ids, got, w_attn_out],
        us=10,
    )
    fwd = add_cores(own, other)
    cot_send = after(cotangent, fwd[1])
    fwd = [after(v, *far) for v in fwd]
    parts = scatter_x(fwd)

    same = [[2 * j + p for j in range(8)] for p in (0, 1)]
    cot_all = lax.all_to_all(cot_send, "band", 0, 0, axis_index_groups=same)
    after_self, a2, cq, cprobs, cross, after_cross, a3 = kernel_call(
        middle_body,
        [
            ((64, 1024), F32),
            chunk,
            ((8, 64, 128), BF),
            ((8, 128, 128), BF),
            ((8, 64, 128), BF),
            ((64, 1024), F32),
            chunk,
        ],
        [ids, text_len, *parts, row(gain_two), row(gain_three), *w_all],
        smem=2,
        mib=60,
        us=10,
    )

    image_c = to_item(after(image_c, fwd[1]))
    a3_own, a3_other = gather_parts(after(a3, image_c))
    dact = dot(after(cot_all, a3).reshape(512, 1024), w_back, 1, 1)
    hid, dpre, da_own, da_other, a3_all = kernel_call(
        hidden_body,
        [((512, 512), BF), ((8, 64, 512), BF), four, four, ((8, 64, 1024), BF)],
        [ids, *a3_own, a3_other, dact, w_hidden],
    )
    both = (da_own.astype(F32) + core_swap(da_other).astype(F32)).astype(BF)
    da3 = swap_x(both)
    quarter = ((4, 64, 1024), BF)
    own, other, dw_back, dw_hidden = kernel_call(
        hidden_grad_body,
        [four, four, ((512, 1024), F32), ((1024, 512), F32)],
        [ids, after(hid, both), dpre, a3_all, cot_all, w_back],
        scratch=[pltpu.VMEM((8, 64, 1024), BF)],
        mib=60,
        us=10,
    )
    dw_back, dw_hidden = lax.psum((dw_back, dw_hidden), "band")
    a2g2, g1_low, g1, cols, dgain23 = kernel_call(
        middle_back_body,
        [((64, 3072), BF), chunk, ((64, 1024), F32), ((8, 192, 256), BF), ((16, 128), F32)],
        [ids, da3, of_tp(after(cot_all, own)), after_cross, after_self, cq, cprobs, cross]
        + [image_c, row(gain_one), row(gain_two), row(gain_three)]
        + w_all,
        scratch=[pltpu.VMEM((64, 1024), F32)],
        mib=60,
    )

    out_both = add_cores(after(own, g1_low), other)
    g1_own = shifts(g1_low)
    g1_other = core_swap(jnp.stack([after(v, *out_both) for v in g1_own]))
    out_parts = scatter_x([after(v, g1_other) for v in out_both])
    (layer_c,) = kernel_call(layer_body, [chunk], [ids, *out_parts, after_cross])
    dq, kv_own, kv_other, g1_all = kernel_call(
        attend_back_body,
        [((8, 64, 128), BF), ((8, 64, 256), F32), ((8, 64, 256), BF), ((8, 64, 1024), BF)],
        [ids, got, probs, w_attn_out, *g1_own, g1_other],
        scratch=[pltpu.VMEM((1024, 128), F32)] * 2 + [pltpu.VMEM((8, 64, 128), BF)],
        mib=60,
    )
    mid_own = shifts(after(a2g2, kv_other))
    kv_got = lax.ppermute(kv_other, "band", [(b, b ^ 1) for b in range(16)])
    recv = lax.all_to_all(after(cols, *g1_own[1:]), "tp", 0, 0)
    tile = ((4, 128, 128), BF)
    t_own, t_other = kernel_call(
        text_body, [tile, tile], [ids, after(recv, kv_other), w_cross_k, w_cross_v], mib=60
    )
    t_parts = scatter_x(add_cores(t_own, t_other))
    t_mine, t_theirs = kernel_call(
        text_pair_body, [((64, 128), F32), ((64, 128), BF)], [ids, *t_parts]
    )
    t_got = lax.ppermute(t_theirs, "band", [(b, b ^ 1) for b in range(16)])
    (tsum,) = kernel_call(text_sum_body, [((80, 128), BF)], [ids, t_mine, t_got, dgain23])
    tall = lax.all_gather(tsum, ("band", "tp"), axis=0, tiled=True)
    dqkv, own, other = kernel_call(
        first_body,
        [((8, 64, 384), BF), four, four],
        [ids, dq, kv_own, kv_got, after(w_query, t_own), w_key, w_value],
    )
    both = add_cores(own, other)
    e1 = scatter_x(both)
    mid_other = core_swap(jnp.stack([after(v, dqkv) for v in mid_own]))
    (grads,) = kernel_call(
        weight_grad_body,
        [((16, 64, 1024), BF)],
        [ids, *mid_own, mid_other, recv, self_cols, g1_all, of_item(text_in)]
        + [after(dqkv, both[1], t_theirs)],
        scratch=[pltpu.VMEM((8, 64, 1024), BF)] * 3,
        mib=60,
    )
    grads_got = lax.all_to_all(
        after(grads, dw_back, dw_hidden, tsum, layer_c, *e1[1:]), "band", 0, 0
    )
    last, dgain1 = kernel_call(
        image_body,
        [((2, 64, 1024), BF), ((8, 128), F32)],
        [ids, *e1, image_c, row(gain_one), after(g1, t_own), layer_c],
        mib=60,
    )
    moved = to_band(last)
    dgain1 = sum_four_places(dgain1, z_shift)

    dw_back, dw_hidden = kernel_call(
        copy_body, [((512, 1024), F32), ((1024, 512), F32)], [ids, dw_back, dw_hidden], mib=60
    )
    grads_got = after(grads_got, dw_back, dw_hidden)
    (ga0,) = kernel_call(sum_body, [chunk], [ids, grads_got], mib=60)
    ga = jnp.stack([ga0] + [z_shift(ga0, k) for k in (1, 2, 3)])
    dgain1 = sum_four_places(after(dgain1, ga0), y_shift)
    ga = after(ga, dgain1, tall)
    ga = [ga] + [y_shift(ga, k) for k in (1, 2, 3)]
    last_all = lax.all_gather(after(moved, grads_got), "tp", axis=0)
    gimg, layer_out = kernel_call(
        place_body,
        [((8, 64, 1024), F32), ((8, 64, 1024), BF)],
        [ids, last_all],
        mib=60,
    )
    dgain1 = sum_four_places(after(dgain1, gimg), x_shift)
    dgain1 = dgain1 + core_swap(dgain1)
    grad_text, dgains = kernel_call(
        text_place_body,
        [((1024, 1024), F32), ((16, 128), F32)],
        [ids, tall],
    )
    dw_query, dw_key, dw_value, dw_cross_q, dw_cross_k, dw_cross_v, dw_attn_out, dw_cross_out = (
        kernel_call(
            place_weights_body,
            [((1024, 128), F32)] * 6 + [((128, 1024), F32)] * 2,
            [ids, after(ga[0], gimg), *ga[1:]],
        )
    )
    return (
        layer_out,
        gimg,
        grad_text.reshape(8, 128, 1024),
        dgain1.reshape(1024),
        dw_query,
        dw_key,
        dw_value,
        dw_attn_out,
        dgains[0:8].reshape(1024),
        dw_cross_q,
        dw_cross_k,
        dw_cross_v,
        dw_cross_out,
        dgains[8:16].reshape(1024),
        dw_hidden,
        dw_back,
    )


def solution(mesh):
    rows, cols, heads = P(None, "band", None), P(None, "tp"), P("tp", None)
    in_specs = (
        rows, P(), P(), rows, P(), cols, cols, cols, heads, P(), cols, cols, cols, heads, P(), cols, heads,
    )
    out_specs = (
        rows, rows, P(), P(), cols, cols, cols, heads, P(), cols, cols, cols, heads, P(), cols, heads,
    )
    return jax.shard_map(local, mesh=mesh, in_specs=in_specs, out_specs=out_specs, check_vma=False)
```

```python
import jax
import jax.numpy as jnp
from jax import lax
from jax.experimental import pallas as pl
from jax.experimental.pallas import tpu as pltpu
from jax.sharding import PartitionSpec as P

HD = 64
norm_eps = 1e-05
mask_fill = -1000000000.0
BF = jnp.bfloat16
F32 = jnp.float32


def dot(a, b, ca, cb):
    return lax.dot_general(a, b, (((ca,), (cb,)), ((), ())), preferred_element_type=F32)


def norm_parts(rows):
    centred = rows - jnp.mean(rows, axis=-1, keepdims=True)
    inv = lax.rsqrt(jnp.mean(centred * centred, axis=-1, keepdims=True) + norm_eps)
    return centred * inv, inv


def norm_back(rows, gain, grad):
    xh, inv = norm_parts(rows)
    eg = grad * gain
    back = inv * (
        eg
        - jnp.mean(eg, axis=-1, keepdims=True)
        - xh * jnp.mean(eg * xh, axis=-1, keepdims=True)
    )
    return back, jnp.sum((grad * xh).reshape(-1, rows.shape[-1]), axis=0)


def x_shift(v, k):
    return lax.ppermute(v, "tp", [(t, (t + 2 * k) % 8) for t in range(8)])


def core_swap(v):
    return lax.ppermute(v, "tp", [(t, t ^ 1) for t in range(8)])


def z_shift(v, k):
    return lax.ppermute(v, "band", [(b, b // 4 * 4 + (b + k) % 4) for b in range(16)])


def y_shift(v, k):
    return lax.ppermute(v, "band", [(b, (b + 4 * k) % 16) for b in range(16)])


def gather_band(v):
    rows = jnp.stack([v] + [z_shift(v, k) for k in (1, 2, 3)])
    return jnp.stack([rows] + [y_shift(rows, k) for k in (1, 2, 3)])


def to_item(v):
    perm = [(c * 8 + i, (2 * i + c % 2) * 8 + c // 2) for c in range(16) for i in range(8)]
    return lax.ppermute(v, ("band", "tp"), perm)


def to_band(v):
    perm = [((2 * i + c % 2) * 8 + c // 2, c * 8 + i) for c in range(16) for i in range(8)]
    return lax.ppermute(v, ("band", "tp"), perm)


def kernel_call(body, outs, args, smem=1, scratch=(), mib=40, us=0):
    def whole(shape):
        return pl.BlockSpec(
            shape, lambda *_: (0,) * len(shape), pipeline_mode=pl.Buffered(buffer_count=1)
        )

    def block(arg):
        if not isinstance(arg, tuple):
            return whole(arg.shape)
        array, first, place = arg
        rest = array.shape[1:]
        return pl.BlockSpec(
            (first, *rest),
            lambda _, *scalars: (place(*scalars), *(0 for _ in rest)),
            pipeline_mode=pl.Buffered(buffer_count=1),
        )

    arrays = [a[0] if isinstance(a, tuple) else a for a in args]
    return pl.pallas_call(
        body,
        out_shape=[jax.ShapeDtypeStruct(s, d) for s, d in outs],
        grid_spec=pltpu.PrefetchScalarGridSpec(
            num_scalar_prefetch=smem,
            grid=(1,),
            in_specs=[block(a) for a in args[smem:]],
            out_specs=[whole(s) for s, _ in outs],
            scratch_shapes=list(scratch),
        ),
        compiler_params=pltpu.CompilerParams(vmem_limit_bytes=mib * 2**20),
        cost_estimate=pl.CostEstimate(
            flops=1, bytes_accessed=1 + us * 3700000, transcendentals=0
        ),
    )(*arrays)


def of_item(v):
    return (v, 1, lambda ids, *_: lax.div(ids[0], 2))


def of_tp(v):
    return (v, 1, lambda ids, *_: ids[1])


def slot(ids, s):
    t = ids[1]
    x = lax.rem(lax.div(t, 2) + 4 - s % 4, 4)
    core = lax.rem(t + s // 4, 2)
    return 2 * x + core


def side(ids, s, x):
    return 2 * x + lax.rem(ids[1] + s, 2)


def band_slot(ids, n):
    y, z = lax.div(ids[0], 4), lax.rem(ids[0], 4)
    return 4 * lax.rem(y + 4 - n // 4, 4) + lax.rem(z + 4 - n % 4, 4)


def head_rows(v):
    first = lax.broadcasted_iota(jnp.int32, v.shape, 1) < 64
    zero = jnp.zeros_like(v)
    return jnp.concatenate([jnp.where(first, v, zero), jnp.where(first, zero, v)], axis=0)


def head_cols(v):
    r = v.shape[0] // 2
    first = lax.broadcasted_iota(jnp.int32, (r, 128), 1) < 64
    return jnp.where(first, v[:r], v[r:])


def soft(s):
    e = jnp.exp(s - jnp.max(s, axis=-1, keepdims=True))
    return (e / jnp.sum(e, axis=-1, keepdims=True)).astype(BF)


def soft_back(p, dp):
    pf = p.astype(F32)
    return (pf * (dp - jnp.sum(dp * pf, axis=-1, keepdims=True))).astype(BF)


def sum_four(e0, e1, e2, e3):
    return (e0[...].astype(F32) + e2[...].astype(F32)) + (
        e1[...].astype(F32) + e3[...].astype(F32)
    )


def fold(v):
    return jnp.concatenate([v[:, 128 * m : 128 * m + 128] for m in range(8)], axis=0)


def qkv_body(ids, image, gain, wq, wk, wv, send, own, a1):
    own[...] = image[ids[1]]
    for i in range(8):
        xh, _ = norm_parts(image[i].astype(F32))
        a1[i * 64 : i * 64 + 64] = (xh * gain[...]).astype(BF)
    w = jnp.concatenate([wq[...], wk[...], wv[...]], axis=1)
    qkv = dot(a1[...], w, 1, 0).astype(BF).reshape(8, 64, 384)
    cols = pl.ds(pl.multiple_of(ids[1] * 128, 128), 128)
    for i in range(8):
        part = image[i, :, cols]
        for p in (0, 1):
            send[2 * i + p, :, 0:384] = qkv[i]
            send[2 * i + p, :, 384:512] = part


def prep_body(ids, text, wcq, wck, wcv, wco, buf):
    mine = text[0]
    buf[:, 0:1024] = jnp.transpose(wcq[...].astype(F32)).astype(BF)
    buf[:, 1024:2048] = wco[...]
    buf[:, 2048:2176] = dot(wck[...], mine, 0, 1).astype(BF)
    buf[:, 2176:2304] = dot(wcv[...], mine, 0, 1).astype(BF)


def attend_body(ids, got, wo, cols, probs, own, other):
    par = lax.rem(ids[0], 2)
    for j in range(8):
        n = 128 * (j + 1)
        q = head_rows(got[2 * j + par, :, 0:128])
        k = got[0 : 2 * j + 2, :, 128:256].reshape(n, 128)
        v = got[0 : 2 * j + 2, :, 256:384].reshape(n, 128)
        s = dot(q, k, 1, 1) * 0.125
        row = lax.broadcasted_iota(jnp.int32, (128, n), 0) % 64 + (128 * j + 64 * par)
        s = jnp.where(lax.broadcasted_iota(jnp.int32, (128, n), 1) <= row, s, mask_fill)
        p = soft(s)
        probs[j, :, 0:n] = p
        cols[j] = head_cols(dot(p, v, 1, 0)).astype(BF)
    mine = pl.ds(pl.multiple_of(ids[1] * 128, 128), 128)
    for ref, first in ((other, 4), (own, 0)):
        c = jnp.concatenate([cols[slot(ids, first + k)] for k in range(4)], axis=0)
        ref[...] = dot(c, wo[...], 1, 0).astype(BF).reshape(4, 64, 1024)
        part = dot(c, wo[:, mine], 1, 0)
        for k in range(4):
            res = got[2 * slot(ids, first + k) + par, :, 384:512].astype(F32)
            ref[k, :, mine] = (part[64 * k : 64 * k + 64] + res).astype(BF)


def attend_back_body(
    ids, got, probs, wo, a0, a1, a2, a3, others, dq, kv_own, kv_other, g1, dk, dv, dheads
):
    par = lax.rem(ids[0], 2)
    for k, a in enumerate((a0, a1, a2, a3)):
        g1[slot(ids, k)] = a[...]
        g1[slot(ids, 4 + k)] = others[k]
    dheads[...] = dot(g1[...].reshape(512, 1024), wo[...], 1, 1).astype(BF).reshape(8, 64, 128)
    dk[...] = jnp.zeros_like(dk)
    dv[...] = jnp.zeros_like(dv)
    for j in range(8):
        n = 128 * (j + 1)
        q = head_rows(got[2 * j + par, :, 0:128])
        k = got[0 : 2 * j + 2, :, 128:256].reshape(n, 128)
        v = got[0 : 2 * j + 2, :, 256:384].reshape(n, 128)
        g = head_rows(dheads[j])
        p = probs[j, :, 0:n]
        ds = soft_back(p, dot(g, v, 1, 1))
        dv[0:n] += dot(p, g, 0, 0)
        dk[0:n] += dot(ds, q, 0, 0)
        dq[j] = (head_cols(dot(ds, k, 1, 0)) * 0.125).astype(BF)
    for j in range(8):
        own = pl.ds(pl.multiple_of(128 * j + 64 * par, 64), 64)
        other = pl.ds(pl.multiple_of(128 * j + 64 - 64 * par, 64), 64)
        kv_own[j, :, 0:128] = dk[own] * 0.125
        kv_own[j, :, 128:256] = dv[own]
        kv_other[j, :, 0:128] = (dk[other] * 0.125).astype(BF)
        kv_other[j, :, 128:256] = dv[other].astype(BF)


def split_weights(refs):
    halves = []
    for first in (0, 5):
        a, b, q, o, c = refs[first : first + 5]
        cut = [(r.at[:, 0:1024], r.at[:, 1024:2304]) for r in (a, b, c)]
        halves += [cut[0], cut[1], (q, o), cut[2]]
    return [h[0] for h in halves], [h[1] for h in halves]


def middle_body(ids, tlen, e0, e1, e2, e3, gain2, gain3, *refs):
    (wq, wo), outs = split_weights(refs[:10]), refs[10:]
    after_self, a2, cq, probs, cross, after_cross, a3 = outs
    acc = sum_four(e0, e1, e2, e3)
    after_self[...] = acc
    xh, _ = norm_parts(acc)
    a2[...] = (xh * gain2[...]).astype(BF)
    live = lax.broadcasted_iota(jnp.int32, (128, 128), 1) < tlen[lax.div(ids[0], 2)]
    for s in range(8):
        cqs = dot(a2[...], wq[s][...], 1, 1).astype(BF)
        cq[s] = cqs
        sc = dot(head_rows(cqs), wo[s][:, 1024:1152], 1, 0) * 0.125
        p = soft(jnp.where(live, sc, mask_fill))
        probs[s] = p
        cross[s] = head_cols(dot(p, wo[s][:, 1152:1280], 1, 1)).astype(BF)
    acc = after_self[...]
    for s in range(8):
        acc += dot(cross[s], wo[s][:, 0:1024], 1, 0)
    after_cross[...] = acc
    xh, _ = norm_parts(acc)
    a3[...] = (xh * gain3[...]).astype(BF)


def middle_back_body(ids, parts, cot, after_cross, after_self, cq, probs, cross, image, gain1, gain2, gain3, *refs):
    (wq, wo), (both, g1_low, g1, cols, dgain, g2) = split_weights(refs[:10]), refs[10:]
    e = sum_four(*(parts.at[x] for x in range(4)))
    back, dg3 = norm_back(after_cross[...], gain3[...], e)
    g2[...] = cot[0].astype(F32) + back
    g2l = g2[...].astype(BF)
    both[:, 1024:2048] = g2l
    xh, _ = norm_parts(image[...].astype(F32))
    both[:, 2048:3072] = (xh * gain1[...]).astype(BF)
    da2 = jnp.zeros((64, 1024), F32)
    for s in range(8):
        dc = head_rows(dot(g2l, wo[s][:, 0:1024], 1, 1).astype(BF))
        p = probs[s]
        ds = soft_back(p, dot(dc, wo[s][:, 1152:1280], 1, 0))
        dq = (head_cols(dot(ds, wo[s][:, 1024:1152], 1, 1)) * 0.125).astype(BF)
        dk = dot(head_rows(cq[s]), ds, 0, 0) * 0.125
        dv = dot(dc, p, 0, 0)
        to = slot(ids, s)
        cols[to, 0:64, 0:128] = cross[s]
        cols[to, 0:64, 128:256] = dq
        cols[to, 64:192, 0:128] = dk.astype(BF)
        cols[to, 64:192, 128:256] = dv.astype(BF)
        da2 += dot(dq, wq[s][...], 1, 0)
    v = after_self[...]
    xh, _ = norm_parts(v)
    both[:, 0:1024] = (xh * gain2[...]).astype(BF)
    back, dg2 = norm_back(v, gain2[...], da2)
    g1[...] = g2[...] + back
    g1l = g1[...].astype(BF)
    g1_low[...] = g1l
    dgain[0:8] = jnp.concatenate([dg2[128 * m : 128 * m + 128].reshape(1, 128) for m in range(8)])
    dgain[8:16] = jnp.concatenate([dg3[128 * m : 128 * m + 128].reshape(1, 128) for m in range(8)])


def hidden_body(ids, a0, a1, a2, a3, others, dact, wh, hid, dpre, da_own, da_other, a3_all):
    for k, a in enumerate((a0, a1, a2, a3)):
        a3_all[slot(ids, k)] = a[...]
        a3_all[slot(ids, 4 + k)] = others[k]
    for r in range(4):
        rows = slice(128 * r, 128 * r + 128)
        u = dot(a3_all[2 * r : 2 * r + 2].reshape(128, 1024), wh[...], 1, 0)
        th = jnp.tanh(0.7978845608028654 * (u + 0.044715 * u * u * u))
        hid[rows] = (0.5 * u * (1.0 + th)).astype(BF)
        slope = 0.5 * (1.0 + th) + 0.5 * u * (1.0 - th * th) * (
            0.7978845608028654 * (1.0 + 0.134145 * u * u)
        )
        dpre[2 * r : 2 * r + 2] = (dact[rows] * slope).astype(BF).reshape(2, 64, 512)
    for ref, s in ((da_other, 1), (da_own, 0)):
        d = jnp.concatenate([dpre[side(ids, s, x)] for x in range(4)], axis=0)
        ref[...] = dot(d, wh[...], 1, 1).astype(BF).reshape(4, 64, 1024)


def hidden_grad_body(ids, hid, dpre, a3_all, cot, wb, own, other, dwb, dwh, part):
    h = hid[...]
    part[...] = dot(h, wb[...], 1, 0).astype(BF).reshape(8, 64, 1024)
    for k in range(4):
        own[k] = part[slot(ids, k)]
        other[k] = part[slot(ids, 4 + k)]
    dwb[...] = dot(h, cot[...].reshape(512, 1024), 0, 0)
    dwh[...] = dot(a3_all[...].reshape(512, 1024), dpre[...].reshape(512, 512), 0, 0)


def first_body(ids, dq, kv_own, kv_got, wq, wk, wv, dqkv, own, other):
    for j in range(8):
        dqkv[j, :, 0:128] = dq[j]
        dqkv[j, :, 128:384] = (kv_own[j] + kv_got[j].astype(F32)).astype(BF)
    w = jnp.concatenate([wq[...], wk[...], wv[...]], axis=1)
    for ref, first in ((other, 4), (own, 0)):
        d = jnp.concatenate([dqkv[slot(ids, first + k)] for k in range(4)], axis=0)
        ref[...] = dot(d, w, 1, 1).astype(BF).reshape(4, 64, 1024)


def copy_body(ids, dwb, dwh, out_b, out_h):
    out_b[...] = dwb[...]
    out_h[...] = dwh[...]


def layer_body(ids, p0, p1, p2, p3, after_cross, out):
    out[...] = (after_cross[...] + sum_four(p0, p1, p2, p3)).astype(BF)


def image_body(ids, e0, e1, e2, e3, image, gain, g1, layer, both, dgain):
    e = sum_four(e0, e1, e2, e3)
    back, dg = norm_back(image[...].astype(F32), gain[...], e)
    both[0] = (g1[...] + back).astype(BF)
    both[1] = layer[...]
    dgain[...] = jnp.concatenate([dg[128 * m : 128 * m + 128].reshape(1, 128) for m in range(8)])


def text_body(ids, recv, wck, wcv, own, other):
    acc = recv[0, 64:192].astype(F32)
    for j in range(1, 8):
        acc += recv[j, 64:192].astype(F32)
    d = acc.astype(BF)
    tp = dot(d[:, 0:128], wck[...], 0, 1) + dot(d[:, 128:256], wcv[...], 0, 1)
    parts = [fold(tp[8 * n : 8 * n + 8]) for n in range(16)]
    rows = [jnp.concatenate([parts[n], parts[8 + n]], axis=0).astype(BF) for n in range(8)]
    all_rows = jnp.concatenate(rows, axis=0).reshape(8, 128, 128)
    for n in range(8):
        x = lax.rem(lax.div(ids[1], 2) + 4 - n // 2, 4)
        core = lax.rem(ids[1] + n % 2, 2)

        @pl.when(core == 0)
        def _():
            own[x] = all_rows[n]

        @pl.when(core == 1)
        def _():
            other[x] = all_rows[n]


def text_pair_body(ids, p0, p1, p2, p3, mine, theirs):
    total = sum_four(p0, p1, p2, p3)
    odd = lax.rem(ids[0], 2) == 1
    mine[...] = jnp.where(odd, total[64:128], total[0:64])
    theirs[...] = jnp.where(odd, total[0:64], total[64:128]).astype(BF)


def weight_grad_body(
    ids,
    a0,
    a1,
    a2,
    a3,
    others,
    recv,
    self_cols,
    g1,
    text,
    dqkv,
    out,
    s1,
    s2,
    sg,
):
    for k, a in enumerate((a0, a1, a2, a3)):
        for to, v in ((slot(ids, k), a[...]), (slot(ids, 4 + k), others[k])):
            s2[to] = v[:, 0:1024]
            sg[to] = v[:, 1024:2048]
            s1[to] = v[:, 2048:3072]
    flat = lambda v: v.reshape(512, v.shape[-1])
    cross, dcq = flat(recv[:, 0:64, 0:128]), flat(recv[:, 0:64, 128:256])
    blocks = lambda v: v.astype(BF).reshape(16, 64, v.shape[-1])
    out[:, :, 0:384] = blocks(dot(flat(s1[...]), flat(dqkv[...]), 0, 0))
    out[:, :, 384:512] = blocks(dot(flat(s2[...]), dcq, 0, 0))
    acc = recv[0, 64:192].astype(F32)
    for j in range(1, 8):
        acc += recv[j, 64:192].astype(F32)
    d = acc.astype(BF)
    out[:, :, 512:640] = blocks(dot(text[0], d[:, 0:128], 0, 1))
    out[:, :, 640:768] = blocks(dot(text[0], d[:, 128:256], 0, 1))
    dao = dot(flat(self_cols[...]), flat(g1[...]), 0, 0)
    dco = dot(cross, flat(sg[...]), 0, 0)
    for b in range(16):
        rows = slice(8 * b, 8 * b + 8)
        out[b, :, 768:896] = fold(dao[rows]).astype(BF)
        out[b, :, 896:1024] = fold(dco[rows]).astype(BF)


def sum_body(ids, got, out):
    acc = got[0].astype(F32)
    for b in range(1, 16):
        acc += got[b].astype(F32)
    out[...] = acc.astype(BF)


def text_sum_body(ids, mine, got, dgain23, out):
    out[0:64] = (mine[...] + got[...].astype(F32)).astype(BF)
    out[64:80] = dgain23[...].astype(BF)


def text_place_body(ids, parts, out, dgain):
    acc = jnp.zeros((16, 128), F32)
    for n in range(128):
        v = parts[80 * n : 80 * n + 80].astype(F32)
        out[8 * n : 8 * n + 8] = jnp.concatenate(
            [v[8 * m : 8 * m + 8] for m in range(8)], axis=1
        )
        acc += v[64:80]
    dgain[...] = acc


def place_body(ids, parts, gimg, layer):
    for t in range(8):
        gimg[t] = parts[t, 0].astype(F32)
        layer[t] = parts[t, 1]


def place_weights_body(ids, p0, p1, p2, p3, o0, o1, o2, o3, o4, o5, o6, o7):
    for n in range(16):
        b = band_slot(ids, n)
        block = (p0, p1, p2, p3)[n // 4][n % 4].astype(F32)
        rows = pl.ds(pl.multiple_of(64 * b, 64), 64)
        for c, o in enumerate((o0, o1, o2, o3, o4, o5)):
            o[rows] = block[:, 128 * c : 128 * c + 128]
        rows = pl.ds(pl.multiple_of(8 * b, 8), 8)
        for c, o in enumerate((o6, o7)):
            cols = block[:, 768 + 128 * c : 896 + 128 * c]
            for m in range(8):
                o[rows, 128 * m : 128 * m + 128] = cols[8 * m : 8 * m + 8]


def after(v, *deps):
    return lax.optimization_barrier((v, *deps))[0]


same_core = [[0, 2, 4, 6], [1, 3, 5, 7]]


def swap_x(v):
    return lax.all_to_all(v, "tp", 0, 0, axis_index_groups=same_core)


def sum_four_places(v, move):
    return (v + move(v, 2)) + (move(v, 1) + move(v, 3))


def shifts(v):
    return [v] + [x_shift(v, k) for k in (1, 2, 3)]


def gather_parts(v):
    own = shifts(v)
    return own, core_swap(jnp.stack(own))


def add_cores(own, other):
    got = core_swap(other)
    return [(own[k].astype(F32) + got[k].astype(F32)).astype(BF) for k in range(4)]


def scatter_x(both):
    return [both[0]] + [x_shift(both[k], -k) for k in (1, 2, 3)]


def local(
    image_in,
    text_in,
    text_len,
    cotangent,
    gain_one,
    w_query,
    w_key,
    w_value,
    w_attn_out,
    gain_two,
    w_cross_q,
    w_cross_k,
    w_cross_v,
    w_cross_out,
    gain_three,
    w_hidden,
    w_back,
):
    ids = jnp.stack([lax.axis_index("band"), lax.axis_index("tp")])
    row = lambda g: g.reshape(1, 1024)
    chunk, four = ((64, 1024), BF), ((4, 64, 1024), BF)

    send, image_c = kernel_call(
        qkv_body,
        [((16, 64, 512), BF), chunk],
        [ids, image_in, row(gain_one), w_query, w_key, w_value],
        scratch=[pltpu.VMEM((512, 1024), BF)],
        mib=60,
    )
    got = lax.all_to_all(send, "band", 0, 0)

    (wbuf,) = kernel_call(
        prep_body,
        [((128, 2304), BF)],
        [ids, of_item(after(text_in, send)), w_cross_q, w_cross_k, w_cross_v, w_cross_out],
        mib=60,
    )
    near = [wbuf, x_shift(wbuf, 1), x_shift(wbuf, 3)]
    far = [x_shift(near[1][:, :1024], 1), x_shift(near[2][:, 1024:], 3)]
    w_own = [near[0], near[1], *far, near[2]]
    w_all = w_own + [core_swap(v) for v in w_own]

    got = after(got, wbuf)
    self_cols, probs, own, other = kernel_call(
        attend_body,
        [((8, 64, 128), BF), ((8, 128, 1024), BF), four, four],
        [ids, got, w_attn_out],
        us=10,
    )
    fwd = add_cores(own, other)
    cot_send = after(cotangent, fwd[1])
    fwd = [after(v, *far) for v in fwd]
    parts = scatter_x(fwd)

    same = [[2 * j + p for j in range(8)] for p in (0, 1)]
    cot_all = lax.all_to_all(cot_send, "band", 0, 0, axis_index_groups=same)
    after_self, a2, cq, cprobs, cross, after_cross, a3 = kernel_call(
        middle_body,
        [
            ((64, 1024), F32),
            chunk,
            ((8, 64, 128), BF),
            ((8, 128, 128), BF),
            ((8, 64, 128), BF),
            ((64, 1024), F32),
            chunk,
        ],
        [ids, text_len, *parts, row(gain_two), row(gain_three), *w_all],
        smem=2,
        mib=60,
        us=10,
    )

    image_c = to_item(after(image_c, fwd[1]))
    a3_own, a3_other = gather_parts(after(a3, image_c))
    dact = dot(after(cot_all, a3).reshape(512, 1024), w_back, 1, 1)
    hid, dpre, da_own, da_other, a3_all = kernel_call(
        hidden_body,
        [((512, 512), BF), ((8, 64, 512), BF), four, four, ((8, 64, 1024), BF)],
        [ids, *a3_own, a3_other, dact, w_hidden],
    )
    both = (da_own.astype(F32) + core_swap(da_other).astype(F32)).astype(BF)
    da3 = swap_x(both)
    quarter = ((4, 64, 1024), BF)
    own, other, dw_back, dw_hidden = kernel_call(
        hidden_grad_body,
        [four, four, ((512, 1024), F32), ((1024, 512), F32)],
        [ids, after(hid, both), dpre, a3_all, cot_all, w_back],
        scratch=[pltpu.VMEM((8, 64, 1024), BF)],
        mib=60,
        us=10,
    )
    dw_back, dw_hidden = lax.psum((dw_back, dw_hidden), "band")
    a2g2, g1_low, g1, cols, dgain23 = kernel_call(
        middle_back_body,
        [((64, 3072), BF), chunk, ((64, 1024), F32), ((8, 192, 256), BF), ((16, 128), F32)],
        [ids, da3, of_tp(after(cot_all, own)), after_cross, after_self, cq, cprobs, cross]
        + [image_c, row(gain_one), row(gain_two), row(gain_three)]
        + w_all,
        scratch=[pltpu.VMEM((64, 1024), F32)],
        mib=60,
    )

    out_both = add_cores(after(own, g1_low), other)
    g1_own = shifts(g1_low)
    g1_other = core_swap(jnp.stack([after(v, *out_both) for v in g1_own]))
    out_parts = scatter_x([after(v, g1_other) for v in out_both])
    (layer_c,) = kernel_call(layer_body, [chunk], [ids, *out_parts, after_cross])
    dq, kv_own, kv_other, g1_all = kernel_call(
        attend_back_body,
        [((8, 64, 128), BF), ((8, 64, 256), F32), ((8, 64, 256), BF), ((8, 64, 1024), BF)],
        [ids, got, probs, w_attn_out, *g1_own, g1_other],
        scratch=[pltpu.VMEM((1024, 128), F32)] * 2 + [pltpu.VMEM((8, 64, 128), BF)],
        mib=60,
    )
    mid_own = shifts(after(a2g2, kv_other))
    kv_got = lax.ppermute(kv_other, "band", [(b, b ^ 1) for b in range(16)])
    recv = lax.all_to_all(after(cols, *g1_own[1:]), "tp", 0, 0)
    tile = ((4, 128, 128), BF)
    t_own, t_other = kernel_call(
        text_body, [tile, tile], [ids, after(recv, kv_other), w_cross_k, w_cross_v], mib=60
    )
    t_parts = scatter_x(add_cores(t_own, t_other))
    t_mine, t_theirs = kernel_call(
        text_pair_body, [((64, 128), F32), ((64, 128), BF)], [ids, *t_parts]
    )
    t_got = lax.ppermute(t_theirs, "band", [(b, b ^ 1) for b in range(16)])
    (tsum,) = kernel_call(text_sum_body, [((80, 128), BF)], [ids, t_mine, t_got, dgain23])
    tall = lax.all_gather(tsum, ("band", "tp"), axis=0, tiled=True)
    dqkv, own, other = kernel_call(
        first_body,
        [((8, 64, 384), BF), four, four],
        [ids, dq, kv_own, kv_got, after(w_query, t_own), w_key, w_value],
    )
    both = add_cores(own, other)
    e1 = scatter_x(both)
    mid_other = core_swap(jnp.stack([after(v, dqkv) for v in mid_own]))
    (grads,) = kernel_call(
        weight_grad_body,
        [((16, 64, 1024), BF)],
        [ids, *mid_own, mid_other, recv, self_cols, g1_all, of_item(text_in)]
        + [after(dqkv, both[1], t_theirs)],
        scratch=[pltpu.VMEM((8, 64, 1024), BF)] * 3,
        mib=60,
    )
    grads_got = lax.all_to_all(
        after(grads, dw_back, dw_hidden, tsum, layer_c, *e1[1:]), "band", 0, 0
    )
    last, dgain1 = kernel_call(
        image_body,
        [((2, 64, 1024), BF), ((8, 128), F32)],
        [ids, *e1, image_c, row(gain_one), after(g1, t_own), layer_c],
        mib=60,
    )
    moved = to_band(last)

    dw_back, dw_hidden = kernel_call(
        copy_body, [((512, 1024), F32), ((1024, 512), F32)], [ids, dw_back, dw_hidden], mib=60
    )
    grads_got = after(grads_got, dw_back, dw_hidden)
    (ga0,) = kernel_call(sum_body, [chunk], [ids, grads_got], mib=60)
    ga = jnp.stack([ga0] + [z_shift(ga0, k) for k in (1, 2, 3)])
    dgain1 = sum_four_places(after(dgain1, ga0), z_shift)
    dgain1 = sum_four_places(dgain1, y_shift)
    ga = after(ga, dgain1, tall)
    ga = [ga] + [y_shift(ga, k) for k in (1, 2, 3)]
    last_all = lax.all_gather(after(moved, grads_got), "tp", axis=0)
    gimg, layer_out = kernel_call(
        place_body,
        [((8, 64, 1024), F32), ((8, 64, 1024), BF)],
        [ids, last_all],
        mib=60,
    )
    dgain1 = sum_four_places(after(dgain1, gimg), x_shift)
    dgain1 = dgain1 + core_swap(dgain1)
    grad_text, dgains = kernel_call(
        text_place_body,
        [((1024, 1024), F32), ((16, 128), F32)],
        [ids, tall],
    )
    dw_query, dw_key, dw_value, dw_cross_q, dw_cross_k, dw_cross_v, dw_attn_out, dw_cross_out = (
        kernel_call(
            place_weights_body,
            [((1024, 128), F32)] * 6 + [((128, 1024), F32)] * 2,
            [ids, after(ga[0], gimg), *ga[1:]],
        )
    )
    return (
        layer_out,
        gimg,
        grad_text.reshape(8, 128, 1024),
        dgain1.reshape(1024),
        dw_query,
        dw_key,
        dw_value,
        dw_attn_out,
        dgains[0:8].reshape(1024),
        dw_cross_q,
        dw_cross_k,
        dw_cross_v,
        dw_cross_out,
        dgains[8:16].reshape(1024),
        dw_hidden,
        dw_back,
    )


def solution(mesh):
    rows, cols, heads = P(None, "band", None), P(None, "tp"), P("tp", None)
    in_specs = (
        rows, P(), P(), rows, P(), cols, cols, cols, heads, P(), cols, cols, cols, heads, P(), cols, heads,
    )
    out_specs = (
        rows, rows, P(), P(), cols, cols, cols, heads, P(), cols, cols, cols, heads, P(), cols, heads,
    )
    return jax.shard_map(local, mesh=mesh, in_specs=in_specs, out_specs=out_specs, check_vma=False)
```
